512 devices in a mesh: gx: 64 (over z, y), gy: 8 (over x, core).
Axes of the slice: x: 4, y: 8, z: 8, core: 2. Of those that a mesh axis runs over, the one named last changes fastest.
Arguments:
- points_x: bfloat16 [262144, 128], P('gx'), may hold values from -40 to 40
- points_y: bfloat16 [65536, 128], P('gy'), may hold values from -1.5 to 1.5
- g_init: float32 [65536], P('gy'), may hold values from -4 to 4
- log_a: float32 [262144], P('gx'), may hold values from -1 to 1
- log_b: float32 [65536], P('gy'), may hold values from -1 to 1
- tile_cols: int32 [512, 16], P('gx'), may hold values from 0 to 127, as said below
- tile_counts: int32 [512], P('gx'), may hold values from 2 to 16, as said below
Outputs:
- row_potential: float32 [262144], P('gx')
- column_potential: float32 [65536], P('gy')
- barycenter: float32 [262144, 128], P('gx')
The draws below stay inside these ranges and needn't reach their ends.
Inputs may be any that keep to these rules, and one draw needn't show every extreme that they name: `tile_cols`: each tile row lists 16 different column tiles; every column tile is the first entry of some tile row. `tile_counts`: some tile row keeps all 16.
All inputs are finite; a program needn't handle non-finite values.
Results may differ from the reference program's by a relative error of at most 0.0034.
Values sent between devices are 32-bit elements; how exact they have to be, the bound alone decides.
A program may use at most 64 MiB of HBM per device.

```python
import jax
import jax.numpy as jnp
from jax import lax

D = 128
TILE = 512
KMAX = 16
NRT = 512
NCT = 128
NX = 262144
NY = 65536


def mask_tables(key):
    key_scores = jax.random.fold_in(key, 201)
    key_first = jax.random.fold_in(key, 202)
    key_one = jax.random.fold_in(key, 203)
    key_two = jax.random.fold_in(key, 204)
    key_full = jax.random.fold_in(key, 205)
    column_ids = jnp.arange(NCT, dtype=jnp.int32)
    scores = jax.random.randint(key_scores, (NRT, NCT), 0, 2 ** 20, dtype=jnp.int32) * NCT + column_ids[None, :]
    first = (jax.random.permutation(key_first, NRT) % NCT).astype(jnp.int32)
    scores = jnp.where(column_ids[None, :] == first[:, None], -1, scores)
    order = jnp.argsort(scores, axis=1, stable=True).astype(jnp.int32)
    cols = order[:, :KMAX]
    count_one = jax.random.randint(key_one, (NRT,), 2, KMAX + 1, dtype=jnp.int32)
    count_two = jax.random.randint(key_two, (NRT,), 2, KMAX + 1, dtype=jnp.int32)
    counts = jnp.minimum(count_one, count_two)
    full_row = jax.random.randint(key_full, (), 0, NRT, dtype=jnp.int32)
    counts = jnp.where(jnp.arange(NRT, dtype=jnp.int32) == full_row, KMAX, counts).astype(jnp.int32)
    return (cols, counts)


def pair_points(key):
    key_base = jax.random.fold_in(key, 301)
    key_extra = jax.random.fold_in(key, 302)
    spread = D ** (-0.25)
    base = jnp.clip(jax.random.normal(key_base, (NY // 2, D), jnp.float32), -4.0, 4.0) * spread
    extra = jnp.clip(jax.random.normal(key_extra, (NY // 2, D), jnp.float32), -4.0, 4.0) * spread
    second = extra
    return jnp.stack([base, second], axis=1).reshape(NY, D)


def draw_tile_cols(key, part):
    return mask_tables(key)[0]


def draw_tile_counts(key, part):
    return mask_tables(key)[1]


def draw_points_y(key, part):
    points = pair_points(key)
    return points.astype(jnp.bfloat16)


def draw_points_x(key, part):
    key = jax.random.fold_in(key, 3)
    spread = D ** (-0.25)
    points = jnp.clip(jax.random.normal(key, (NX, D), jnp.float32), -4.0, 4.0) * spread
    points = jnp.clip(points, -40.0, 40.0)
    return points.astype(jnp.bfloat16)


def steps_of(stream_key, dims, cuts, smallest, high):
    loudness = 1.0
    for axis_at, blocks in cuts:
        heights = jax.random.uniform(jax.random.fold_in(jax.random.fold_in(stream_key, 6), axis_at), (blocks,), jnp.float32, smallest / len(cuts), high / len(cuts))
        loudness = loudness * jnp.repeat(jnp.exp(heights), dims[axis_at] // blocks).reshape((-1,) + (1,) * (len(dims) - 1 - axis_at))
    return loudness


def gaussian(key, dims, deviation, bound, pieces=(), held_as=jnp.bfloat16):
    gain = steps_of(key, dims, pieces, -0.22, 0.18) if pieces else 1.0
    entries = jax.random.normal(key, dims, jnp.float32) * deviation * gain
    return jnp.minimum(jnp.maximum(entries, -bound), bound).astype(held_as)


def setup_inputs(seed: int = 0) -> dict:
    arg_keys = jax.random.split(jax.random.key(seed), 8)
    points_x = draw_points_x(jax.random.fold_in(arg_keys[7], 71), 0)
    points_y = draw_points_y(jax.random.fold_in(arg_keys[7], 71), 0)
    g_init = gaussian(arg_keys[2], (NY,), 1.0, 4.0, ((0, 8),), jnp.float32)
    log_a = jnp.clip(jax.random.uniform(arg_keys[3], (NX,), jnp.float32, -1.0, 1.0) * steps_of(arg_keys[3], (NX,), ((0, 64),), -0.4, 0.0), -1.0, 1.0)
    log_b = jnp.clip(jax.random.uniform(arg_keys[4], (NY,), jnp.float32, -1.0, 1.0) * steps_of(arg_keys[4], (NY,), ((0, 8),), -0.4, 0.0), -1.0, 1.0)
    tile_cols = draw_tile_cols(jax.random.fold_in(arg_keys[7], 71), 0)
    tile_counts = draw_tile_counts(jax.random.fold_in(arg_keys[7], 71), 0)
    return {"points_x": points_x, "points_y": points_y, "g_init": g_init, "log_a": log_a, "log_b": log_b, "tile_cols": tile_cols, "tile_counts": tile_counts}


EPSILON = 0.5
INV_EPS = 2.0
NEG_FILL = -1.0e30


def reference(points_x, points_y, g_init, log_a, log_b, tile_cols, tile_counts):
    x_tiles = points_x.reshape(NRT, TILE, D)
    y_tiles = points_y.reshape(NCT, TILE, D)
    g_start = g_init.reshape(NCT, TILE)
    kept = jnp.arange(KMAX, dtype=jnp.int32)[None, :] < tile_counts[:, None]

    def tile_products(x_block, cols):
        y_block = y_tiles[cols]
        dots = jnp.einsum("id,kjd->kij", x_block.astype(jnp.float32), y_block.astype(jnp.float32))
        return dots, y_block

    def row_pass(args):
        x_block, cols, keep = args
        dots, unused_block = tile_products(x_block, cols)
        logits = (g_start[cols][:, None, :] + dots) * INV_EPS
        logits = jnp.where(keep[:, None, None], logits, NEG_FILL)
        peak = jnp.max(logits, axis=(0, 2))
        terms = jnp.where(keep[:, None, None], jnp.exp(logits - peak[None, :, None]), 0.0)
        return peak + jnp.log(jnp.sum(terms, axis=(0, 2)))

    row_lse = lax.map(row_pass, (x_tiles, tile_cols, kept))
    f_pot = EPSILON * (log_a.reshape(NRT, TILE) - row_lse)

    def column_step(carry, args):
        peak_all, mass_all = carry
        x_block, cols, keep, f_block = args
        dots, unused_block = tile_products(x_block, cols)
        logits = (f_block[None, :, None] + dots) * INV_EPS
        tile_peak = jnp.max(logits, axis=1)
        tile_mass = jnp.sum(jnp.exp(logits - tile_peak[:, None, :]), axis=1)
        old_peak = peak_all[cols]
        old_mass = mass_all[cols]
        new_peak = jnp.maximum(old_peak, tile_peak)
        new_mass = old_mass * jnp.exp(old_peak - new_peak) + tile_mass * jnp.exp(tile_peak - new_peak)
        new_peak = jnp.where(keep[:, None], new_peak, old_peak)
        new_mass = jnp.where(keep[:, None], new_mass, old_mass)
        return (peak_all.at[cols].set(new_peak), mass_all.at[cols].set(new_mass)), None

    start = (jnp.full((NCT, TILE), NEG_FILL, jnp.float32), jnp.zeros((NCT, TILE), jnp.float32))
    (peak_all, mass_all), unused_out = lax.scan(column_step, start, (x_tiles, tile_cols, kept, f_pot))
    g_pot = EPSILON * (log_b.reshape(NCT, TILE) - (peak_all + jnp.log(mass_all)))

    def bary_pass(args):
        x_block, cols, keep, f_block = args
        dots, y_block = tile_products(x_block, cols)
        logits = (f_block[None, :, None] + g_pot[cols][:, None, :] + dots) * INV_EPS
        weights = jnp.where(keep[:, None, None], jnp.exp(logits), 0.0)
        denom = jnp.sum(weights, axis=(0, 2))
        rounded = lax.optimization_barrier(weights.astype(jnp.bfloat16))
        numer = jnp.einsum("kij,kjd->id", rounded.astype(jnp.float32), y_block.astype(jnp.float32))
        return numer / denom[:, None]

    barycenter = lax.map(bary_pass, (x_tiles, tile_cols, kept, f_pot))
    return f_pot.reshape(NX), g_pot.reshape(NY), barycenter.reshape(NX, D)
```

```python
import functools

import jax
import jax.numpy as jnp
from jax import lax
from jax.experimental import pallas as pl
from jax.experimental.pallas import tpu as pltpu
from jax.sharding import PartitionSpec as P

TILE = 512
LANES = 128
CHUNKS = TILE // LANES
MESH = pl.DeviceIdType.MESH
NEG_FILL = -1e30
SCALE = 2.8853900817779268
VMEM = pl.BlockSpec(memory_space=pltpu.VMEM)
SMEM = pl.BlockSpec(memory_space=pltpu.SMEM)
VMEM_LIMIT = 40 * 1024 * 1024


def params(**kw):
    return pltpu.CompilerParams(vmem_limit_bytes=VMEM_LIMIT, **kw)


def split3(value):
    high = value.astype(jnp.bfloat16).astype(jnp.float32)
    rest = value - high
    middle = rest.astype(jnp.bfloat16).astype(jnp.float32)
    low = (rest - middle).astype(jnp.bfloat16).astype(jnp.float32)
    return [high, middle, low]


def tile_rows(ref, tiles):
    return jnp.concatenate(
        [ref[pl.ds(q, tiles, stride=CHUNKS), :] for q in range(CHUNKS)], axis=1
    )


def as_columns(pieces):
    rows = sum(piece.shape[0] for piece in pieces)
    pieces = pieces + [jnp.zeros((LANES - rows, TILE), jnp.float32)]
    return jnp.concatenate(pieces, axis=0).T.astype(jnp.bfloat16)


def lane_mask(first, period, which):
    lane = lax.broadcasted_iota(jnp.int32, (1, LANES), 1) - first
    hit = (lane == which) | (lane == which + period) | (lane == which + 2 * period)
    return jnp.where(hit, 1.0, 0.0)


def spread(row):
    return jnp.broadcast_to(row, (TILE, LANES)).astype(jnp.bfloat16)


def tile_at(ref, index):
    return ref[pl.ds(pl.multiple_of(index * TILE, TILE), TILE), :]


def product(left, right):
    return lax.dot_general(
        left, right, (((1,), (1,)), ((), ())), preferred_element_type=jnp.float32
    )


def lse_pass(list_ref, live, pick, outer_ref, inner_ref, pot_tiles, columns, peak, mass):
    peak[...] = jnp.full_like(peak, NEG_FILL)
    mass[...] = jnp.zeros_like(mass)

    def step(at, carry):
        outer, inner = pick(list_ref[at])
        left = jnp.concatenate([tile_at(outer_ref, outer), columns[...]], axis=1)
        right = jnp.concatenate(
            [tile_at(inner_ref, inner), spread(lane_mask(0, pot_tiles, outer))], axis=1
        )
        half = TILE // 2
        for part in range(2):
            lanes = slice(part * half, (part + 1) * half)
            sums = product(left, right[lanes, :]).reshape(TILE // 8, 8, half)
            before = peak[inner, :, lanes]
            top = jnp.maximum(before, jnp.max(sums, axis=0))
            terms = jnp.sum(jnp.exp2((sums - top[None]) * SCALE), axis=0)
            mass[inner, :, lanes] = mass[inner, :, lanes] * jnp.exp2((before - top) * SCALE) + terms
            peak[inner, :, lanes] = top
        return carry

    lax.fori_loop(0, live, step, 0)


def lse_finish(peak, mass, out_ref):
    for tile in range(peak.shape[0]):
        top = jnp.max(peak[tile], axis=0, keepdims=True)
        total = jnp.sum(mass[tile] * jnp.exp2((peak[tile] - top) * SCALE), axis=0, keepdims=True)
        lse = jnp.where(total > 0.0, 2.0 * top + jnp.log(total), NEG_FILL)
        for q in range(CHUNKS):
            out_ref[pl.ds(tile * CHUNKS + q, 1), :] = lse[:, q * LANES : (q + 1) * LANES]


def row_kernel(cols_ref, counts_ref, x_ref, y_ref, g_ref, lse_ref, list_ref, columns, peak, mass):
    row_tiles, most = cols_ref.shape
    col_tiles = y_ref.shape[0] // TILE
    me = lax.axis_index("gy")
    live = jnp.int32(0)
    for row in range(row_tiles):
        count = counts_ref[row]
        for slot in range(most):
            at = cols_ref[row, slot] - me * col_tiles
            owned = (at >= 0) & (at < col_tiles) & (slot < count)
            list_ref[live] = row * col_tiles + at
            live = live + jnp.where(owned, 1, 0)
    list_ref[row_tiles * most] = live
    columns[...] = as_columns(split3(tile_rows(g_ref, col_tiles)))
    pick = lambda pair: (lax.rem(pair, col_tiles), lax.div(pair, col_tiles))
    lse_pass(list_ref, live, pick, y_ref, x_ref, col_tiles, columns, peak, mass)
    lse_finish(peak, mass, lse_ref)


def column_kernel(list_ref, x_ref, y_ref, f_ref, lse_ref, columns, peak, mass):
    row_tiles = x_ref.shape[0] // TILE
    col_tiles = y_ref.shape[0] // TILE
    live = list_ref[list_ref.shape[0] - 1]
    columns[...] = as_columns(split3(tile_rows(f_ref, row_tiles)))
    pick = lambda pair: (lax.div(pair, col_tiles), lax.rem(pair, col_tiles))
    lse_pass(list_ref, live, pick, x_ref, y_ref, row_tiles, columns, peak, mass)
    lse_finish(peak, mass, lse_ref)


def bary_kernel(list_ref, x_ref, y_ref, f_ref, g_ref, out_ref, columns):
    row_tiles = x_ref.shape[0] // TILE
    col_tiles = y_ref.shape[0] // TILE
    width = x_ref.shape[1]
    live = list_ref[list_ref.shape[0] - 1]
    first = 3 * col_tiles
    pots = split3(tile_rows(g_ref, col_tiles)) + split3(tile_rows(f_ref, row_tiles))
    columns[...] = as_columns(pots)
    out_ref[...] = jnp.zeros_like(out_ref)

    def step(at, carry):
        pair = list_ref[at]
        row, col = lax.div(pair, col_tiles), lax.rem(pair, col_tiles)
        lane = lax.broadcasted_iota(jnp.int32, (1, LANES), 1)
        of_g = spread(jnp.where(lane < first, 1.0, 0.0))
        of_f = spread(jnp.where(lane < first, 0.0, 1.0))
        y_tile = tile_at(y_ref, col)
        pot = columns[...]
        left = jnp.concatenate(
            [y_tile, pot * of_g + spread(lane_mask(first, row_tiles, row))], axis=1
        )
        right = jnp.concatenate(
            [tile_at(x_ref, row), pot * of_f + spread(lane_mask(0, col_tiles, col))], axis=1
        )
        half = TILE // 2
        for part in range(2):
            lanes = slice(part * half, (part + 1) * half)
            weights = jnp.exp2(product(left, right[lanes, :]) * SCALE)
            out_ref[row, width:, lanes] += jnp.sum(weights.reshape(TILE // 8, 8, half), axis=0)
            out_ref[row, :width, lanes] += lax.dot_general(
                y_tile,
                weights.astype(jnp.bfloat16),
                (((0,), (0,)), ((), ())),
                preferred_element_type=jnp.float32,
            )
        return carry

    lax.fori_loop(0, live, step, 0)


def meet(peers):
    barrier = pltpu.get_barrier_semaphore()
    for peer in peers:
        pl.semaphore_signal(barrier, inc=1, device_id=peer, device_id_type=MESH)
    pl.semaphore_wait(barrier, len(peers))


def send(src, dst, send_sem, recv_sem, peer):
    copy = pltpu.make_async_remote_copy(
        src_ref=src,
        dst_ref=dst,
        send_sem=send_sem,
        recv_sem=recv_sem,
        device_id=peer,
        device_id_type=MESH,
    )
    copy.start()
    return copy


def join(parts):
    top = parts[0]
    for part in parts[1:]:
        top = jnp.maximum(top, part)
    total = jnp.exp(parts[0] - top)
    for part in parts[1:]:
        total = total + jnp.exp(part - top)
    return top + jnp.log(total)


def row_join_kernel(n, lse_ref, log_a_ref, f_ref, held, send_sem, recv_sem):
    me = lax.axis_index("gy")
    peers = [{"gy": lax.rem(me + d, n)} for d in range(1, n)]
    meet(peers)
    copies = [
        send(lse_ref, held.at[me], send_sem.at[i], recv_sem.at[i], peer)
        for i, peer in enumerate(peers)
    ]
    held[me] = lse_ref[...]
    for copy in copies:
        copy.wait()
    f_ref[...] = 0.5 * (log_a_ref[...] - join([held[k] for k in range(n)]))


def col_join_kernel(
    nz, ny, lse_ref, log_b_ref, g_ref, first, part, second, send_sem, recv_sem
):
    me = lax.axis_index("gx")
    z, y = lax.div(me, ny), lax.rem(me, ny)
    y_places = [lax.rem(y + d, ny) for d in range(1, ny)]
    y_peers = [{"gx": z * ny + at} for at in y_places]
    z_peers = [{"gx": lax.rem(z + d, nz) * ny + y} for d in range(1, nz)]
    meet(y_peers + z_peers)
    copies = [
        send(lse_ref.at[at], first.at[i], send_sem.at[i], recv_sem.at[i], peer)
        for i, (at, peer) in enumerate(zip(y_places, y_peers))
    ]
    for copy in copies:
        copy.wait()
    part[...] = join([lse_ref[y]] + [first[i] for i in range(ny - 1)])
    base = ny - 1
    copies = [
        send(part, second.at[z], send_sem.at[base + i], recv_sem.at[base + i], peer)
        for i, peer in enumerate(z_peers)
    ]
    second[z] = part[...]
    for copy in copies:
        copy.wait()
    g_ref[y] = 0.5 * (log_b_ref[y] - join([second[k] for k in range(nz)]))
    base = ny - 1 + nz - 1
    copies = [
        send(g_ref.at[y], g_ref.at[y], send_sem.at[base + i], recv_sem.at[base + i], peer)
        for i, peer in enumerate(y_peers)
    ]
    for copy in copies:
        copy.wait()


def bary_join_kernel(n, part_ref, out_ref, near, far, send_sem, recv_sem):
    me = lax.axis_index("gy")
    chips = n // 2
    chip, core = lax.div(me, 2), lax.rem(me, 2)
    other = 1 - core
    width = out_ref.shape[1]
    sibling = {"gy": chip * 2 + other}
    places = [lax.rem(chip + d, chips) for d in range(chips)]
    peers = [{"gy": at * 2 + core} for at in places]
    meet([sibling] + peers[1:])

    order = [2, 1, 3, 0]
    inside = {
        d: send(
            part_ref.at[places[d] * 2 + other], near.at[d], send_sem.at[d], recv_sem.at[d], sibling
        )
        for d in order
    }
    across = {}
    for d in order:
        inside[d].wait()
        near[d] = near[d] + part_ref[places[d] * 2 + core]
        if d > 0:
            across[d] = send(
                near.at[d], far.at[d - 1], send_sem.at[4 + d], recv_sem.at[4 + d], peers[d]
            )
    total = near[0]
    for d in (1, 3, 2):
        across[d].wait()
        total = total + far[d - 1]
    ratio = total[:width] / jnp.sum(total[width:], axis=0, keepdims=True)
    mine = out_ref.at[pl.ds(pl.multiple_of(me * TILE, TILE), TILE)]
    mine[...] = ratio.T
    gathered = {
        d: send(mine, mine, send_sem.at[8 + d], recv_sem.at[8 + d], peers[d]) for d in (2, 1, 3)
    }
    handed = [send(mine, mine, send_sem.at[8], recv_sem.at[8], sibling)]
    for d in (1, 3, 2):
        gathered[d].wait()
        source = lax.rem(chip - d + chips, chips) * 2 + core
        block = out_ref.at[pl.ds(pl.multiple_of(source * TILE, TILE), TILE)]
        handed.append(send(block, block, send_sem.at[12 + d], recv_sem.at[12 + d], sibling))
    for copy in handed:
        copy.wait()


def local(gx_size, gy_size, points_x, points_y, g_init, log_a, log_b, tile_cols, tile_counts):
    row_tiles, most = tile_cols.shape
    rows, width = points_x.shape
    cols = points_y.shape[0]
    col_tiles = cols // TILE
    nz = 1
    while nz * nz < gx_size:
        nz *= 2
    ny = gx_size // nz
    f32, i32, bf16 = jnp.float32, jnp.int32, jnp.bfloat16
    row_shape, col_shape = (rows // LANES, LANES), (cols // LANES, LANES)
    block = (cols // LANES // ny, LANES)
    dma = pltpu.SemaphoreType.DMA

    def lse_scratch(tiles):
        return [
            pltpu.VMEM((TILE, LANES), bf16),
            pltpu.VMEM((tiles, 8, TILE), f32),
            pltpu.VMEM((tiles, 8, TILE), f32),
        ]

    row_lse, pairs = pl.pallas_call(
        row_kernel,
        out_shape=(
            jax.ShapeDtypeStruct(row_shape, f32),
            jax.ShapeDtypeStruct((row_tiles * most + 1,), i32),
        ),
        in_specs=[SMEM, SMEM, VMEM, VMEM, VMEM],
        out_specs=(VMEM, SMEM),
        scratch_shapes=lse_scratch(row_tiles),
        compiler_params=params(),
        name="row_pass",
    )(tile_cols, tile_counts, points_x, points_y, g_init.reshape(col_shape))

    f_pot = pl.pallas_call(
        functools.partial(row_join_kernel, gy_size),
        out_shape=jax.ShapeDtypeStruct(row_shape, f32),
        in_specs=[VMEM, VMEM],
        out_specs=VMEM,
        scratch_shapes=[
            pltpu.VMEM((gy_size,) + row_shape, f32),
            dma((gy_size - 1,)),
            dma((gy_size - 1,)),
        ],
        compiler_params=params(collective_id=0, has_side_effects=True),
        name="row_join",
    )(row_lse, log_a.reshape(row_shape))

    col_lse = pl.pallas_call(
        column_kernel,
        out_shape=jax.ShapeDtypeStruct(col_shape, f32),
        in_specs=[SMEM, VMEM, VMEM, VMEM],
        out_specs=VMEM,
        scratch_shapes=lse_scratch(col_tiles),
        compiler_params=params(),
        name="column_pass",
    )(pairs, points_x, points_y, f_pot)

    links = 2 * (ny - 1) + nz - 1
    g_pot = pl.pallas_call(
        functools.partial(col_join_kernel, nz, ny),
        out_shape=jax.ShapeDtypeStruct((ny,) + block, f32),
        in_specs=[VMEM, VMEM],
        out_specs=VMEM,
        scratch_shapes=[
            pltpu.VMEM((ny - 1,) + block, f32),
            pltpu.VMEM(block, f32),
            pltpu.VMEM((nz,) + block, f32),
            dma((links,)),
            dma((links,)),
        ],
        compiler_params=params(collective_id=1, has_side_effects=True),
        name="column_join",
    )(col_lse.reshape((ny,) + block), log_b.reshape((ny,) + block))

    partial = pl.pallas_call(
        bary_kernel,
        out_shape=jax.ShapeDtypeStruct((row_tiles, width + 8, TILE), f32),
        in_specs=[SMEM, VMEM, VMEM, VMEM, VMEM],
        out_specs=VMEM,
        scratch_shapes=[pltpu.VMEM((TILE, LANES), bf16)],
        compiler_params=params(),
        name="bary_pass",
    )(pairs, points_x, points_y, f_pot, g_pot.reshape(col_shape))

    barycenter = pl.pallas_call(
        functools.partial(bary_join_kernel, gy_size),
        out_shape=jax.ShapeDtypeStruct((rows, width), f32),
        in_specs=[VMEM],
        out_specs=VMEM,
        scratch_shapes=[
            pltpu.VMEM((4, width + 8, TILE), f32),
            pltpu.VMEM((3, width + 8, TILE), f32),
            dma((16,)),
            dma((16,)),
        ],
        compiler_params=params(collective_id=2, has_side_effects=True),
        name="bary_join",
    )(partial)
    return (f_pot.reshape(-1), g_pot.reshape(-1), barycenter)


def solution(mesh):
    in_specs = (P("gx", None), P("gy", None), P("gy"), P("gx"), P("gy"), P("gx", None), P("gx"))
    out_specs = (P("gx"), P("gy"), P("gx", None))
    body = functools.partial(local, mesh.shape["gx"], mesh.shape["gy"])
    return jax.shard_map(body, mesh=mesh, in_specs=in_specs, out_specs=out_specs, check_vma=False)
```

```python
import functools

import jax
import jax.numpy as jnp
from jax import lax
from jax.experimental import pallas as pl
from jax.experimental.pallas import tpu as pltpu
from jax.sharding import PartitionSpec as P

TILE = 512
LANES = 128
CHUNKS = TILE // LANES
LSE_GROUP = 2
BARY_GROUP = 3
PIECES = 2
MESH = pl.DeviceIdType.MESH
NEG_FILL = -1e30
SCALE = 2.8853900817779268
VMEM = pl.BlockSpec(memory_space=pltpu.VMEM)
SMEM = pl.BlockSpec(memory_space=pltpu.SMEM)
HBM = pl.BlockSpec(memory_space=pltpu.HBM)
VMEM_LIMIT = 40 * 1024 * 1024


def params(**kw):
    return pltpu.CompilerParams(vmem_limit_bytes=VMEM_LIMIT, **kw)


def split3(value):
    high = value.astype(jnp.bfloat16).astype(jnp.float32)
    rest = value - high
    middle = rest.astype(jnp.bfloat16).astype(jnp.float32)
    low = (rest - middle).astype(jnp.bfloat16).astype(jnp.float32)
    return [high, middle, low]


def tile_rows(ref, tiles):
    return jnp.concatenate(
        [ref[pl.ds(q, tiles, stride=CHUNKS), :] for q in range(CHUNKS)], axis=1
    )


def as_columns(pieces):
    rows = sum(piece.shape[0] for piece in pieces)
    pieces = pieces + [jnp.zeros((LANES - rows, TILE), jnp.float32)]
    return jnp.concatenate(pieces, axis=0).T.astype(jnp.bfloat16)


def lane_mask(first, period, which):
    lane = lax.broadcasted_iota(jnp.int32, (1, LANES), 1) - first
    hit = (lane == which) | (lane == which + period) | (lane == which + 2 * period)
    return jnp.where(hit, 1.0, 0.0)


def spread(row):
    return jnp.broadcast_to(row, (TILE, LANES)).astype(jnp.bfloat16)


def tile_at(ref, index):
    return ref[pl.ds(pl.multiple_of(index * TILE, TILE), TILE), :]


def product(left, right):
    return lax.dot_general(
        left, right, (((1,), (1,)), ((), ())), preferred_element_type=jnp.float32
    )


def pair_at(list_ref, live, at):
    return list_ref[jnp.minimum(at, live - 1)]


def pipelined(size, live, fill, drain, add=None):
    groups = lax.div(live + (size - 1), size)

    def step(group, carry):
        if add is not None:
            add(group - 1)
        drain(group)
        fill(group + 1)
        return carry

    if add is None:

        @pl.when(groups > 0)
        def _():
            fill(0)
            lax.fori_loop(0, groups - 1, step, 0)
            drain(groups - 1)

        return

    @pl.when(groups > 1)
    def _():
        fill(0)
        drain(0)
        fill(1)
        lax.fori_loop(1, groups - 1, step, 0)
        add(groups - 2)
        drain(groups - 1)
        add(groups - 1)

    @pl.when(groups == 1)
    def _():
        fill(0)
        drain(0)
        add(0)


def fold_rows(value, op):
    rows, lanes = value.shape
    return op(op(value.reshape(4, rows // 32, 8, lanes), axis=1), axis=0)


def lse_pass(
    list_ref, live, pick, outer_ref, inner_ref, pot_tiles, columns, peak, mass, sums, tops
):
    peak[...] = jnp.full_like(peak, NEG_FILL)
    mass[...] = jnp.zeros_like(mass)
    spare = peak.shape[0] - 1

    def fill(group):
        for u in range(LSE_GROUP):
            outer, inner = pick(pair_at(list_ref, live, group * LSE_GROUP + u))
            left = jnp.concatenate([tile_at(outer_ref, outer), columns[...]], axis=1)
            right = jnp.concatenate(
                [tile_at(inner_ref, inner), spread(lane_mask(0, pot_tiles, outer))], axis=1
            )
            value = product(left, right)
            sums[u] = value
            tops[u] = fold_rows(value, jnp.max)

    def drain(group):
        for u in range(LSE_GROUP):
            at = group * LSE_GROUP + u
            inner = jnp.where(at < live, pick(pair_at(list_ref, live, at))[1], spare)
            before = peak[inner]
            top = jnp.maximum(before, tops[u])
            value = sums[u].reshape(TILE // 8, 8, TILE) - top[None]
            terms = fold_rows(jnp.exp2(value * SCALE).reshape(TILE, TILE), jnp.sum)
            mass[inner] = mass[inner] * jnp.exp2((before - top) * SCALE) + terms
            peak[inner] = top

    pipelined(LSE_GROUP, live, fill, drain)


def lse_finish(peak, mass, out_ref):
    for tile in range(peak.shape[0] - 1):
        top = jnp.max(peak[tile], axis=0, keepdims=True)
        total = jnp.sum(mass[tile] * jnp.exp2((peak[tile] - top) * SCALE), axis=0, keepdims=True)
        lse = jnp.where(total > 0.0, 2.0 * top + jnp.log(total), NEG_FILL)
        for q in range(CHUNKS):
            out_ref[pl.ds(tile * CHUNKS + q, 1), :] = lse[:, q * LANES : (q + 1) * LANES]


def list_kernel(col_tiles, cols_ref, counts_ref, list_ref):
    row_tiles, most = cols_ref.shape
    me = lax.axis_index("gy")
    live = jnp.int32(0)
    for row in range(row_tiles):
        count = counts_ref[row]
        for slot in range(most):
            at = cols_ref[row, slot] - me * col_tiles
            owned = (at >= 0) & (at < col_tiles) & (slot < count)
            list_ref[live] = row * col_tiles + at
            live = live + jnp.where(owned, 1, 0)
    list_ref[row_tiles * most] = live


def row_kernel(list_ref, x_ref, y_ref, g_ref, lse_ref, columns, *sums):
    col_tiles = y_ref.shape[0] // TILE
    live = list_ref[list_ref.shape[0] - 1]
    columns[...] = as_columns(split3(tile_rows(g_ref, col_tiles)))
    pick = lambda pair: (lax.rem(pair, col_tiles), lax.div(pair, col_tiles))
    lse_pass(list_ref, live, pick, y_ref, x_ref, col_tiles, columns, *sums)
    lse_finish(*sums[:2], lse_ref)


def column_kernel(list_ref, x_ref, y_ref, f_ref, lse_ref, columns, *sums):
    row_tiles = x_ref.shape[0] // TILE
    col_tiles = y_ref.shape[0] // TILE
    live = list_ref[list_ref.shape[0] - 1]
    columns[...] = as_columns(split3(tile_rows(f_ref, row_tiles)))
    pick = lambda pair: (lax.div(pair, col_tiles), lax.rem(pair, col_tiles))
    lse_pass(list_ref, live, pick, x_ref, y_ref, row_tiles, columns, *sums)
    lse_finish(*sums[:2], lse_ref)


def bary_kernel(
    list_ref,
    x_ref,
    y_ref,
    f_ref,
    g_ref,
    out_ref,
    f_hbm,
    g_hbm,
    columns,
    pots_g,
    pots_f,
    sums,
    rounded,
    sems,
):
    results = [
        pltpu.make_async_copy(f_ref, f_hbm, sems.at[0]),
        pltpu.make_async_copy(g_ref, g_hbm, sems.at[1]),
    ]
    for copy in results:
        copy.start()
    row_tiles = x_ref.shape[0] // TILE
    col_tiles = y_ref.shape[0] // TILE
    width = x_ref.shape[1]
    live = list_ref[list_ref.shape[0] - 1]
    first = 3 * col_tiles
    pots = split3(tile_rows(g_ref, col_tiles)) + split3(tile_rows(f_ref, row_tiles))
    columns[...] = as_columns(pots)
    out_ref[...] = jnp.zeros_like(out_ref)

    spare = out_ref.shape[0] - 1
    lane = lax.broadcasted_iota(jnp.int32, (1, LANES), 1)
    of_g = spread(jnp.where(lane < first, 1.0, 0.0))
    of_f = spread(jnp.where(lane < first, 0.0, 1.0))
    pots_g[...] = columns[...] * of_g
    pots_f[...] = columns[...] * of_f
    pick = lambda pair: (lax.div(pair, col_tiles), lax.rem(pair, col_tiles))

    def fill(group):
        for u in range(BARY_GROUP):
            row, col = pick(pair_at(list_ref, live, group * BARY_GROUP + u))
            left = jnp.concatenate(
                [tile_at(y_ref, col), pots_g[...] + spread(lane_mask(first, row_tiles, row))],
                axis=1,
            )
            right = jnp.concatenate(
                [tile_at(x_ref, row), pots_f[...] + spread(lane_mask(0, col_tiles, col))], axis=1
            )
            sums[u] = product(left, right)

    def drain(group):
        for u in range(BARY_GROUP):
            at = group * BARY_GROUP + u
            row = jnp.where(at < live, pick(pair_at(list_ref, live, at))[0], spare)
            weights = jnp.exp2(sums[u] * SCALE)
            out_ref[row, width:] += fold_rows(weights, jnp.sum)
            rounded[u] = weights.astype(jnp.bfloat16)

    def add(group):
        for u in range(BARY_GROUP):
            at = group * BARY_GROUP + u
            row, col = pick(pair_at(list_ref, live, at))
            row = jnp.where(at < live, row, spare)
            out_ref[row, :width] += lax.dot_general(
                tile_at(y_ref, col),
                rounded[u],
                (((0,), (0,)), ((), ())),
                preferred_element_type=jnp.float32,
            )

    pipelined(BARY_GROUP, live, fill, drain, add)
    for copy in results:
        copy.wait()


def meet(peers):
    barrier = pltpu.get_barrier_semaphore()
    for peer in peers:
        pl.semaphore_signal(barrier, inc=1, device_id=peer, device_id_type=MESH)
    pl.semaphore_wait(barrier, len(peers))


def send(src, dst, send_sem, recv_sem, peer):
    copy = pltpu.make_async_remote_copy(
        src_ref=src,
        dst_ref=dst,
        send_sem=send_sem,
        recv_sem=recv_sem,
        device_id=peer,
        device_id_type=MESH,
    )
    copy.start()
    return copy


def join(parts):
    top = parts[0]
    for part in parts[1:]:
        top = jnp.maximum(top, part)
    total = jnp.exp(parts[0] - top)
    for part in parts[1:]:
        total = total + jnp.exp(part - top)
    return top + jnp.log(total)


def row_join_kernel(n, lse_ref, log_a_ref, f_ref, held, send_sem, recv_sem):
    me = lax.axis_index("gy")
    peers = [{"gy": lax.rem(me + d, n)} for d in range(1, n)]
    meet(peers)
    copies = [
        send(lse_ref, held.at[me], send_sem.at[i], recv_sem.at[i], peer)
        for i, peer in enumerate(peers)
    ]
    held[me] = lse_ref[...]
    for copy in copies:
        copy.wait()
    f_ref[...] = 0.5 * (log_a_ref[...] - join([held[k] for k in range(n)]))


def col_join_kernel(nz, ny, lse_ref, log_b_ref, g_ref, first, part, second, sems):
    me = lax.axis_index("gx")
    z, y = lax.div(me, ny), lax.rem(me, ny)
    y_peers = [{"gx": z * ny + lax.rem(y + d, ny)} for d in range(1, ny)]
    z_peers = [{"gx": lax.rem(z + d, nz) * ny + y} for d in range(1, nz)]
    meet(y_peers + z_peers)
    half = lse_ref.shape[0] // 2
    n = ny
    for stage in range(2):
        held = (first, second)[stage]
        copies = []
        for upper in range(2):
            own = lse_ref.at[pl.ds(upper * half, half)] if stage == 0 else part.at[upper]
            along_y = upper == stage
            at = y if along_y else z
            for i, peer in enumerate(y_peers if along_y else z_peers):
                k = (stage * 2 + upper) * (n - 1) + i
                copies.append(send(own, held.at[upper, at], sems.at[0, k], sems.at[1, k], peer))
            held[upper, at] = own[...]
        for copy in copies:
            copy.wait()
        for upper in range(2):
            joined = join([held[upper, k] for k in range(n)])
            if stage == 0:
                part[upper] = joined
            else:
                rows = slice(upper * half, (upper + 1) * half)
                g_ref[rows] = 0.5 * (log_b_ref[rows] - joined)


def bary_join_kernel(n, part_ref, out_ref, near, relay, left_in, right_in, sems):
    me = lax.axis_index("gy")
    chips = n // 2
    chip, core = lax.div(me, 2), lax.rem(me, 2)
    other = 1 - core
    width = out_ref.shape[1]
    split = width // 2
    low, high = slice(0, split), slice(split, width + 8)
    places = [lax.rem(chip + d, chips) for d in range(chips)]
    sibling = {"gy": chip * 2 + other}
    right, left = {"gy": places[1] * 2 + core}, {"gy": places[3] * 2 + core}
    meet([sibling, right, left])
    used = [0]

    def go(src, dst, peer):
        k = used[0]
        used[0] += 1
        return send(src, dst, sems.at[0, k], sems.at[1, k], peer)

    pieces = [slice(k * TILE // PIECES, (k + 1) * TILE // PIECES) for k in range(PIECES)]
    inside = {d: go(part_ref.at[places[d] * 2 + other], near.at[d], sibling) for d in (2, 1, 3, 0)}
    waits = []

    def add_inside(d):
        inside[d].wait()
        near[d] = near[d] + part_ref[places[d] * 2 + core]

    add_inside(2)
    far = []
    for piece in pieces:
        far.append(
            (
                go(near.at[2, low, piece], relay.at[low, piece], right),
                go(near.at[2, high, piece], relay.at[high, piece], left),
            )
        )
    add_inside(1)
    add_inside(3)
    direct, passed = [], []
    for k, piece in enumerate(pieces):
        direct.append(
            (
                go(near.at[1, high, piece], left_in.at[high, piece], right),
                go(near.at[3, low, piece], right_in.at[low, piece], left),
            )
        )
        if k == 0:
            add_inside(0)
        far[k][0].wait()
        near[1, low, piece] = near[1, low, piece] + relay[low, piece]
        to_right = go(near.at[1, low, piece], left_in.at[low, piece], right)
        far[k][1].wait()
        near[3, high, piece] = near[3, high, piece] + relay[high, piece]
        to_left = go(near.at[3, high, piece], right_in.at[high, piece], left)
        passed.append((to_right, to_left))

    def rows_of(place, kind, first, count):
        start = (place * 2 + kind) * TILE + first
        return out_ref.at[pl.ds(pl.multiple_of(start, 8), count)]

    size = TILE // PIECES
    own = []
    for k, piece in enumerate(pieces):
        for copy in direct[k] + passed[k]:
            copy.wait()
        total = near[0, :, piece] + left_in[:, piece] + right_in[:, piece]
        ratio = total[:width] / jnp.sum(total[width:], axis=0, keepdims=True)
        mine = rows_of(chip, core, k * size, size)
        mine[...] = ratio.T
        own.append((go(mine, mine, right), go(mine, mine, left)))
        waits.append(go(mine, mine, sibling))
    onward = []
    for k in range(PIECES):
        for side in range(2):
            own[k][side].wait()
            place = places[3] if side == 0 else places[1]
            block = rows_of(place, core, k * size + side * size // 2, size // 2)
            onward.append((k, side, go(block, block, right if side == 0 else left)))
            block = rows_of(place, core, k * size, size)
            waits.append(go(block, block, sibling))
    for k, side, copy in onward:
        copy.wait()
        block = rows_of(places[2], core, k * size + side * size // 2, size // 2)
        waits.append(go(block, block, sibling))
    for copy in waits:
        copy.wait()


def local(gx_size, gy_size, points_x, points_y, g_init, log_a, log_b, tile_cols, tile_counts):
    row_tiles, most = tile_cols.shape
    rows, width = points_x.shape
    cols = points_y.shape[0]
    col_tiles = cols // TILE
    nz = 1
    while nz * nz < gx_size:
        nz *= 2
    ny = gx_size // nz
    f32, i32, bf16 = jnp.float32, jnp.int32, jnp.bfloat16
    row_shape, col_shape = (rows // LANES, LANES), (cols // LANES, LANES)
    dma = pltpu.SemaphoreType.DMA

    def lse_scratch(tiles):
        return [
            pltpu.VMEM((TILE, LANES), bf16),
            pltpu.VMEM((tiles + 1, 8, TILE), f32),
            pltpu.VMEM((tiles + 1, 8, TILE), f32),
            pltpu.VMEM((LSE_GROUP, TILE, TILE), f32),
            pltpu.VMEM((LSE_GROUP, 8, TILE), f32),
        ]

    pairs = pl.pallas_call(
        functools.partial(list_kernel, col_tiles),
        out_shape=jax.ShapeDtypeStruct((row_tiles * most + 1,), i32),
        in_specs=[SMEM, SMEM],
        out_specs=SMEM,
        compiler_params=params(),
        name="list_pairs",
    )(tile_cols, tile_counts)

    row_lse = pl.pallas_call(
        row_kernel,
        out_shape=jax.ShapeDtypeStruct(row_shape, f32),
        in_specs=[SMEM, VMEM, VMEM, VMEM],
        out_specs=VMEM,
        scratch_shapes=lse_scratch(row_tiles),
        compiler_params=params(),
        name="row_pass",
    )(pairs, points_x, points_y, g_init.reshape(col_shape))

    f_pot = pl.pallas_call(
        functools.partial(row_join_kernel, gy_size),
        out_shape=jax.ShapeDtypeStruct(row_shape, f32),
        in_specs=[VMEM, VMEM],
        out_specs=VMEM,
        scratch_shapes=[
            pltpu.VMEM((gy_size,) + row_shape, f32),
            dma((gy_size - 1,)),
            dma((gy_size - 1,)),
        ],
        compiler_params=params(collective_id=0, has_side_effects=True),
        name="row_join",
    )(row_lse, log_a.reshape(row_shape))

    col_lse = pl.pallas_call(
        column_kernel,
        out_shape=jax.ShapeDtypeStruct(col_shape, f32),
        in_specs=[SMEM, VMEM, VMEM, VMEM],
        out_specs=VMEM,
        scratch_shapes=lse_scratch(col_tiles),
        compiler_params=params(),
        name="column_pass",
    )(pairs, points_x, points_y, f_pot)

    half = (2, col_shape[0] // 2, LANES)
    g_pot = pl.pallas_call(
        functools.partial(col_join_kernel, nz, ny),
        out_shape=jax.ShapeDtypeStruct(col_shape, f32),
        in_specs=[VMEM, VMEM],
        out_specs=VMEM,
        scratch_shapes=[
            pltpu.VMEM((2, ny) + half[1:], f32),
            pltpu.VMEM(half, f32),
            pltpu.VMEM((2, ny) + half[1:], f32),
            dma((2, 4 * (ny - 1))),
        ],
        compiler_params=params(collective_id=1, has_side_effects=True),
        name="column_join",
    )(col_lse, log_b.reshape(col_shape))

    partial, f_pot, g_pot = pl.pallas_call(
        bary_kernel,
        out_shape=(
            jax.ShapeDtypeStruct((row_tiles + 1, width + 8, TILE), f32),
            jax.ShapeDtypeStruct(row_shape, f32),
            jax.ShapeDtypeStruct(col_shape, f32),
        ),
        in_specs=[SMEM, VMEM, VMEM, VMEM, VMEM],
        out_specs=(VMEM, HBM, HBM),
        scratch_shapes=[pltpu.VMEM((TILE, LANES), bf16)] * 3
        + [
            pltpu.VMEM((BARY_GROUP, TILE, TILE), f32),
            pltpu.VMEM((BARY_GROUP, TILE, TILE), bf16),
            dma((2,)),
        ],
        compiler_params=params(),
        name="bary_pass",
    )(pairs, points_x, points_y, f_pot, g_pot)

    barycenter = pl.pallas_call(
        functools.partial(bary_join_kernel, gy_size),
        out_shape=jax.ShapeDtypeStruct((rows, width), f32),
        in_specs=[VMEM],
        out_specs=VMEM,
        scratch_shapes=[pltpu.VMEM((4, width + 8, TILE), f32)]
        + [pltpu.VMEM((width + 8, TILE), f32)] * 3
        + [dma((2, 4 + 15 * PIECES))],
        compiler_params=params(collective_id=2, has_side_effects=True),
        name="bary_join",
    )(partial)
    return (f_pot.reshape(-1), g_pot.reshape(-1), barycenter)


def solution(mesh):
    in_specs = (P("gx", None), P("gy", None), P("gy"), P("gx"), P("gy"), P("gx", None), P("gx"))
    out_specs = (P("gx"), P("gy"), P("gx", None))
    body = functools.partial(local, mesh.shape["gx"], mesh.shape["gy"])
    return jax.shard_map(body, mesh=mesh, in_specs=in_specs, out_specs=out_specs, check_vma=False)
```

```python
import functools

import jax
import jax.numpy as jnp
from jax import lax
from jax.experimental import pallas as pl
from jax.experimental.pallas import tpu as pltpu
from jax.sharding import PartitionSpec as P

TILE = 512
LANES = 128
CHUNKS = TILE // LANES
LSE_GROUP = 2
BARY_GROUP = 3
PIECES = 4
MESH = pl.DeviceIdType.MESH
NEG_FILL = -1e30
SCALE = 2.8853900817779268
VMEM = pl.BlockSpec(memory_space=pltpu.VMEM)
SMEM = pl.BlockSpec(memory_space=pltpu.SMEM)
HBM = pl.BlockSpec(memory_space=pltpu.HBM)
VMEM_LIMIT = 40 * 1024 * 1024


def params(**kw):
    return pltpu.CompilerParams(vmem_limit_bytes=VMEM_LIMIT, **kw)


def split3(value):
    high = value.astype(jnp.bfloat16).astype(jnp.float32)
    rest = value - high
    middle = rest.astype(jnp.bfloat16).astype(jnp.float32)
    low = (rest - middle).astype(jnp.bfloat16).astype(jnp.float32)
    return [high, middle, low]


def tile_rows(ref, tiles):
    return jnp.concatenate(
        [ref[pl.ds(q, tiles, stride=CHUNKS), :] for q in range(CHUNKS)], axis=1
    )


def as_columns(pieces):
    rows = sum(piece.shape[0] for piece in pieces)
    pieces = pieces + [jnp.zeros((LANES - rows, TILE), jnp.float32)]
    return jnp.concatenate(pieces, axis=0).T.astype(jnp.bfloat16)


def lane_mask(first, period, which):
    lane = lax.broadcasted_iota(jnp.int32, (1, LANES), 1) - first
    hit = (lane == which) | (lane == which + period) | (lane == which + 2 * period)
    return jnp.where(hit, 1.0, 0.0)


def spread(row):
    return jnp.broadcast_to(row, (TILE, LANES)).astype(jnp.bfloat16)


def tile_at(ref, index):
    return ref[pl.ds(pl.multiple_of(index * TILE, TILE), TILE), :]


def product(left, right):
    return lax.dot_general(
        left, right, (((1,), (1,)), ((), ())), preferred_element_type=jnp.float32
    )


def pair_at(list_ref, live, at):
    return list_ref[jnp.minimum(at, live - 1)]


def pipelined(size, live, fill, drain, add=None):
    groups = lax.div(live + (size - 1), size)

    def step(group, carry):
        if add is not None:
            add(group - 1)
        drain(group)
        fill(group + 1)
        return carry

    if add is None:

        @pl.when(groups > 0)
        def _():
            fill(0)
            lax.fori_loop(0, groups - 1, step, 0)
            drain(groups - 1)

        return

    @pl.when(groups > 1)
    def _():
        fill(0)
        drain(0)
        fill(1)
        lax.fori_loop(1, groups - 1, step, 0)
        add(groups - 2)
        drain(groups - 1)
        add(groups - 1)

    @pl.when(groups == 1)
    def _():
        fill(0)
        drain(0)
        add(0)


def fold_rows(value, op):
    rows, lanes = value.shape
    return op(op(value.reshape(4, rows // 32, 8, lanes), axis=1), axis=0)


def lse_pass(
    list_ref, live, pick, outer_ref, inner_ref, pot_tiles, columns, peak, mass, sums, tops
):
    peak[...] = jnp.full_like(peak, NEG_FILL)
    mass[...] = jnp.zeros_like(mass)
    spare = peak.shape[0] - 1

    def fill(group):
        for u in range(LSE_GROUP):
            outer, inner = pick(pair_at(list_ref, live, group * LSE_GROUP + u))
            left = jnp.concatenate([tile_at(outer_ref, outer), columns[...]], axis=1)
            right = jnp.concatenate(
                [tile_at(inner_ref, inner), spread(lane_mask(0, pot_tiles, outer))], axis=1
            )
            value = product(left, right)
            sums[u] = value
            tops[u] = fold_rows(value, jnp.max)

    def drain(group):
        for u in range(LSE_GROUP):
            at = group * LSE_GROUP + u
            inner = jnp.where(at < live, pick(pair_at(list_ref, live, at))[1], spare)
            before = peak[inner]
            top = jnp.maximum(before, tops[u])
            value = sums[u].reshape(TILE // 8, 8, TILE) - top[None]
            terms = fold_rows(jnp.exp2(value * SCALE).reshape(TILE, TILE), jnp.sum)
            mass[inner] = mass[inner] * jnp.exp2((before - top) * SCALE) + terms
            peak[inner] = top

    pipelined(LSE_GROUP, live, fill, drain)


def lse_finish(peak, mass, out_ref):
    for tile in range(peak.shape[0] - 1):
        top = jnp.max(peak[tile], axis=0, keepdims=True)
        total = jnp.sum(mass[tile] * jnp.exp2((peak[tile] - top) * SCALE), axis=0, keepdims=True)
        lse = jnp.where(total > 0.0, 2.0 * top + jnp.log(total), NEG_FILL)
        for q in range(CHUNKS):
            out_ref[pl.ds(tile * CHUNKS + q, 1), :] = lse[:, q * LANES : (q + 1) * LANES]


def row_kernel(
    cols_hbm,
    counts_hbm,
    g_hbm,
    y_hbm,
    x_hbm,
    lse_ref,
    list_ref,
    x_ref,
    y_ref,
    cols_ref,
    counts_ref,
    g_ref,
    sems,
    columns,
    *sums,
):
    arrivals = [(cols_hbm, cols_ref), (counts_hbm, counts_ref), (g_hbm, g_ref)]
    arrivals += [(y_hbm, y_ref), (x_hbm, x_ref)]
    copies = [
        pltpu.make_async_copy(src, dst, sems.at[i]) for i, (src, dst) in enumerate(arrivals)
    ]
    for copy in copies:
        copy.start()
    row_tiles, most = cols_ref.shape
    col_tiles = y_ref.shape[0] // TILE
    me = lax.axis_index("gy")
    for copy in copies[:3]:
        copy.wait()
    columns[...] = as_columns(split3(tile_rows(g_ref, col_tiles)))
    live = jnp.int32(0)
    for row in range(row_tiles):
        count = counts_ref[row]
        base = (row - me) * col_tiles
        for slot in range(most):
            pair = cols_ref[row, slot] + base
            owned = (pair >= row * col_tiles) & (pair < (row + 1) * col_tiles) & (slot < count)
            list_ref[live] = pair
            live = live + jnp.where(owned, 1, 0)
    list_ref[row_tiles * most] = live
    copies[3].wait()
    copies[4].wait()
    pick = lambda pair: (lax.rem(pair, col_tiles), lax.div(pair, col_tiles))
    lse_pass(list_ref, live, pick, y_ref, x_ref, col_tiles, columns, *sums)
    lse_finish(*sums[:2], lse_ref)


def column_kernel(list_ref, x_ref, y_ref, f_ref, lse_ref, columns, *sums):
    row_tiles = x_ref.shape[0] // TILE
    col_tiles = y_ref.shape[0] // TILE
    live = list_ref[list_ref.shape[0] - 1]
    columns[...] = as_columns(split3(tile_rows(f_ref, row_tiles)))
    pick = lambda pair: (lax.div(pair, col_tiles), lax.rem(pair, col_tiles))
    lse_pass(list_ref, live, pick, x_ref, y_ref, row_tiles, columns, *sums)
    lse_finish(*sums[:2], lse_ref)


def bary_kernel(
    list_ref,
    x_ref,
    y_ref,
    f_ref,
    g_ref,
    out_ref,
    f_hbm,
    g_hbm,
    columns,
    pots_g,
    pots_f,
    sums,
    rounded,
    sems,
):
    results = [
        pltpu.make_async_copy(f_ref, f_hbm, sems.at[0]),
        pltpu.make_async_copy(g_ref, g_hbm, sems.at[1]),
    ]
    for copy in results:
        copy.start()
    row_tiles = x_ref.shape[0] // TILE
    col_tiles = y_ref.shape[0] // TILE
    width = x_ref.shape[1]
    live = list_ref[list_ref.shape[0] - 1]
    first = 3 * col_tiles
    pots = split3(tile_rows(g_ref, col_tiles)) + split3(tile_rows(f_ref, row_tiles))
    columns[...] = as_columns(pots)
    out_ref[...] = jnp.zeros_like(out_ref)

    spare = out_ref.shape[0] - 1
    lane = lax.broadcasted_iota(jnp.int32, (1, LANES), 1)
    of_g = spread(jnp.where(lane < first, 1.0, 0.0))
    of_f = spread(jnp.where(lane < first, 0.0, 1.0))
    pots_g[...] = columns[...] * of_g
    pots_f[...] = columns[...] * of_f
    pick = lambda pair: (lax.div(pair, col_tiles), lax.rem(pair, col_tiles))

    def fill(group):
        for u in range(BARY_GROUP):
            row, col = pick(pair_at(list_ref, live, group * BARY_GROUP + u))
            left = jnp.concatenate(
                [tile_at(y_ref, col), pots_g[...] + spread(lane_mask(first, row_tiles, row))],
                axis=1,
            )
            right = jnp.concatenate(
                [tile_at(x_ref, row), pots_f[...] + spread(lane_mask(0, col_tiles, col))], axis=1
            )
            sums[u] = product(left, right)

    def drain(group):
        for u in range(BARY_GROUP):
            at = group * BARY_GROUP + u
            row = jnp.where(at < live, pick(pair_at(list_ref, live, at))[0], spare)
            weights = jnp.exp2(sums[u] * SCALE)
            out_ref[row, width:] += fold_rows(weights, jnp.sum)
            rounded[u] = weights.astype(jnp.bfloat16)

    def add(group):
        for u in range(BARY_GROUP):
            at = group * BARY_GROUP + u
            row, col = pick(pair_at(list_ref, live, at))
            row = jnp.where(at < live, row, spare)
            out_ref[row, :width] += lax.dot_general(
                tile_at(y_ref, col),
                rounded[u],
                (((0,), (0,)), ((), ())),
                preferred_element_type=jnp.float32,
            )

    pipelined(BARY_GROUP, live, fill, drain, add)
    for copy in results:
        copy.wait()


def meet(peers):
    barrier = pltpu.get_barrier_semaphore()
    for peer in peers:
        pl.semaphore_signal(barrier, inc=1, device_id=peer, device_id_type=MESH)
    pl.semaphore_wait(barrier, len(peers))


def send(src, dst, send_sem, recv_sem, peer):
    copy = pltpu.make_async_remote_copy(
        src_ref=src,
        dst_ref=dst,
        send_sem=send_sem,
        recv_sem=recv_sem,
        device_id=peer,
        device_id_type=MESH,
    )
    copy.start()
    return copy


def join(parts):
    top = parts[0]
    for part in parts[1:]:
        top = jnp.maximum(top, part)
    total = jnp.exp(parts[0] - top)
    for part in parts[1:]:
        total = total + jnp.exp(part - top)
    return top + jnp.log(total)


def row_join_kernel(n, lse_ref, log_a_ref, f_ref, held, send_sem, recv_sem):
    me = lax.axis_index("gy")
    peers = [{"gy": lax.rem(me + d, n)} for d in range(1, n)]
    meet(peers)
    copies = [
        send(lse_ref, held.at[me], send_sem.at[i], recv_sem.at[i], peer)
        for i, peer in enumerate(peers)
    ]
    held[me] = lse_ref[...]
    for copy in copies:
        copy.wait()
    f_ref[...] = 0.5 * (log_a_ref[...] - join([held[k] for k in range(n)]))


def col_join_kernel(nz, ny, lse_ref, log_b_ref, g_ref, first, part, second, sems):
    me = lax.axis_index("gx")
    z, y = lax.div(me, ny), lax.rem(me, ny)
    y_peers = [{"gx": z * ny + lax.rem(y + d, ny)} for d in range(1, ny)]
    z_peers = [{"gx": lax.rem(z + d, nz) * ny + y} for d in range(1, nz)]
    meet(y_peers + z_peers)
    half = lse_ref.shape[0] // 2
    n = ny
    for stage in range(2):
        held = (first, second)[stage]
        copies = []
        for upper in range(2):
            own = lse_ref.at[pl.ds(upper * half, half)] if stage == 0 else part.at[upper]
            along_y = upper == stage
            at = y if along_y else z
            for i, peer in enumerate(y_peers if along_y else z_peers):
                k = (stage * 2 + upper) * (n - 1) + i
                copies.append(send(own, held.at[upper, at], sems.at[0, k], sems.at[1, k], peer))
            held[upper, at] = own[...]
        for copy in copies:
            copy.wait()
        for upper in range(2):
            joined = join([held[upper, k] for k in range(n)])
            if stage == 0:
                part[upper] = joined
            else:
                rows = slice(upper * half, (upper + 1) * half)
                g_ref[rows] = 0.5 * (log_b_ref[rows] - joined)


def bary_join_kernel(n, part_ref, out_ref, near, relay, left_in, right_in, sems):
    me = lax.axis_index("gy")
    chips = n // 2
    chip, core = lax.div(me, 2), lax.rem(me, 2)
    other = 1 - core
    width = out_ref.shape[1]
    split = width // 2
    low, high = slice(0, split), slice(split, width + 8)
    places = [lax.rem(chip + d, chips) for d in range(chips)]
    sibling = {"gy": chip * 2 + other}
    right, left = {"gy": places[1] * 2 + core}, {"gy": places[3] * 2 + core}
    meet([sibling, right, left])
    used = [0]

    def go(src, dst, peer):
        k = used[0]
        used[0] += 1
        return send(src, dst, sems.at[0, k], sems.at[1, k], peer)

    pieces = [slice(k * TILE // PIECES, (k + 1) * TILE // PIECES) for k in range(PIECES)]
    inside = {d: go(part_ref.at[places[d] * 2 + other], near.at[d], sibling) for d in (2, 1, 3, 0)}
    waits = []

    def add_inside(d):
        inside[d].wait()
        near[d] = near[d] + part_ref[places[d] * 2 + core]

    add_inside(2)
    far = []
    for piece in pieces:
        far.append(
            (
                go(near.at[2, low, piece], relay.at[low, piece], right),
                go(near.at[2, high, piece], relay.at[high, piece], left),
            )
        )
    add_inside(1)
    add_inside(3)
    direct, passed = [], []
    for k, piece in enumerate(pieces):
        direct.append(
            (
                go(near.at[1, high, piece], left_in.at[high, piece], right),
                go(near.at[3, low, piece], right_in.at[low, piece], left),
            )
        )
        if k == 0:
            add_inside(0)
        far[k][0].wait()
        near[1, low, piece] = near[1, low, piece] + relay[low, piece]
        to_right = go(near.at[1, low, piece], left_in.at[low, piece], right)
        far[k][1].wait()
        near[3, high, piece] = near[3, high, piece] + relay[high, piece]
        to_left = go(near.at[3, high, piece], right_in.at[high, piece], left)
        passed.append((to_right, to_left))

    def rows_of(place, kind, first, count):
        start = (place * 2 + kind) * TILE + first
        return out_ref.at[pl.ds(pl.multiple_of(start, 8), count)]

    size = TILE // PIECES
    own = []
    for k, piece in enumerate(pieces):
        for copy in direct[k] + passed[k]:
            copy.wait()
        total = near[0, :, piece] + left_in[:, piece] + right_in[:, piece]
        ratio = total[:width] / jnp.sum(total[width:], axis=0, keepdims=True)
        mine = rows_of(chip, core, k * size, size)
        mine[...] = ratio.T
        own.append((go(mine, mine, right), go(mine, mine, left)))
        waits.append(go(mine, mine, sibling))
    onward = []
    for k in range(PIECES):
        for side in range(2):
            own[k][side].wait()
            place = places[3] if side == 0 else places[1]
            block = rows_of(place, core, k * size + side * size // 2, size // 2)
            onward.append((k, side, go(block, block, right if side == 0 else left)))
            block = rows_of(place, core, k * size, size)
            waits.append(go(block, block, sibling))
    for k, side, copy in onward:
        copy.wait()
        block = rows_of(places[2], core, k * size + side * size // 2, size // 2)
        waits.append(go(block, block, sibling))
    for copy in waits:
        copy.wait()


def local(gx_size, gy_size, points_x, points_y, g_init, log_a, log_b, tile_cols, tile_counts):
    row_tiles, most = tile_cols.shape
    rows, width = points_x.shape
    cols = points_y.shape[0]
    col_tiles = cols // TILE
    nz = 1
    while nz * nz < gx_size:
        nz *= 2
    ny = gx_size // nz
    f32, i32, bf16 = jnp.float32, jnp.int32, jnp.bfloat16
    row_shape, col_shape = (rows // LANES, LANES), (cols // LANES, LANES)
    dma = pltpu.SemaphoreType.DMA

    def lse_scratch(tiles):
        return [
            pltpu.VMEM((TILE, LANES), bf16),
            pltpu.VMEM((tiles + 1, 8, TILE), f32),
            pltpu.VMEM((tiles + 1, 8, TILE), f32),
            pltpu.VMEM((LSE_GROUP, TILE, TILE), f32),
            pltpu.VMEM((LSE_GROUP, 8, TILE), f32),
        ]

    sources = (tile_cols, tile_counts, g_init.reshape(col_shape), points_y, points_x)
    row_lse, pairs, points_x, points_y = pl.pallas_call(
        row_kernel,
        out_shape=(
            pltpu.VMEM(row_shape, f32),
            jax.ShapeDtypeStruct((row_tiles * most + 1,), i32),
            pltpu.VMEM(points_x.shape, bf16),
            pltpu.VMEM(points_y.shape, bf16),
        ),
        in_specs=[HBM] * 5,
        out_specs=(VMEM, SMEM, VMEM, VMEM),
        scratch_shapes=[
            pltpu.SMEM(tile_cols.shape, i32),
            pltpu.SMEM(tile_counts.shape, i32),
            pltpu.VMEM(col_shape, f32),
            dma((5,)),
        ]
        + lse_scratch(row_tiles),
        compiler_params=params(),
        name="row_pass",
    )(*[pltpu.with_memory_space_constraint(source, pltpu.HBM) for source in sources])

    f_pot = pl.pallas_call(
        functools.partial(row_join_kernel, gy_size),
        out_shape=jax.ShapeDtypeStruct(row_shape, f32),
        in_specs=[VMEM, VMEM],
        out_specs=VMEM,
        scratch_shapes=[
            pltpu.VMEM((gy_size,) + row_shape, f32),
            dma((gy_size - 1,)),
            dma((gy_size - 1,)),
        ],
        compiler_params=params(collective_id=0, has_side_effects=True),
        name="row_join",
    )(row_lse, log_a.reshape(row_shape))

    col_lse = pl.pallas_call(
        column_kernel,
        out_shape=jax.ShapeDtypeStruct(col_shape, f32),
        in_specs=[SMEM, VMEM, VMEM, VMEM],
        out_specs=VMEM,
        scratch_shapes=lse_scratch(col_tiles),
        compiler_params=params(),
        name="column_pass",
    )(pairs, points_x, points_y, f_pot)

    half = (2, col_shape[0] // 2, LANES)
    g_pot = pl.pallas_call(
        functools.partial(col_join_kernel, nz, ny),
        out_shape=jax.ShapeDtypeStruct(col_shape, f32),
        in_specs=[VMEM, VMEM],
        out_specs=VMEM,
        scratch_shapes=[
            pltpu.VMEM((2, ny) + half[1:], f32),
            pltpu.VMEM(half, f32),
            pltpu.VMEM((2, ny) + half[1:], f32),
            dma((2, 4 * (ny - 1))),
        ],
        compiler_params=params(collective_id=1, has_side_effects=True),
        name="column_join",
    )(col_lse, log_b.reshape(col_shape))

    partial, f_pot, g_pot = pl.pallas_call(
        bary_kernel,
        out_shape=(
            jax.ShapeDtypeStruct((row_tiles + 1, width + 8, TILE), f32),
            jax.ShapeDtypeStruct(row_shape, f32),
            jax.ShapeDtypeStruct(col_shape, f32),
        ),
        in_specs=[SMEM, VMEM, VMEM, VMEM, VMEM],
        out_specs=(VMEM, HBM, HBM),
        scratch_shapes=[pltpu.VMEM((TILE, LANES), bf16)] * 3
        + [
            pltpu.VMEM((BARY_GROUP, TILE, TILE), f32),
            pltpu.VMEM((BARY_GROUP, TILE, TILE), bf16),
            dma((2,)),
        ],
        compiler_params=params(),
        name="bary_pass",
    )(pairs, points_x, points_y, f_pot, g_pot)

    barycenter = pl.pallas_call(
        functools.partial(bary_join_kernel, gy_size),
        out_shape=jax.ShapeDtypeStruct((rows, width), f32),
        in_specs=[VMEM],
        out_specs=VMEM,
        scratch_shapes=[pltpu.VMEM((4, width + 8, TILE), f32)]
        + [pltpu.VMEM((width + 8, TILE), f32)] * 3
        + [dma((2, 4 + 15 * PIECES))],
        compiler_params=params(collective_id=2, has_side_effects=True),
        name="bary_join",
    )(partial)
    return (f_pot.reshape(-1), g_pot.reshape(-1), barycenter)


def solution(mesh):
    in_specs = (P("gx", None), P("gy", None), P("gy"), P("gx"), P("gy"), P("gx", None), P("gx"))
    out_specs = (P("gx"), P("gy"), P("gx", None))
    body = functools.partial(local, mesh.shape["gx"], mesh.shape["gy"])
    return jax.shard_map(body, mesh=mesh, in_specs=in_specs, out_specs=out_specs, check_vma=False)
```

```python
import functools

import jax
import jax.numpy as jnp
from jax import lax
from jax.experimental import pallas as pl
from jax.experimental.pallas import tpu as pltpu
from jax.sharding import PartitionSpec as P

TILE = 512
LANES = 128
CHUNKS = TILE // LANES
LSE_GROUP = 2
BARY_GROUP = 2
PIECES = 4
PIECE = TILE // PIECES
PIECE_LANES = [slice(k * PIECE, (k + 1) * PIECE) for k in range(PIECES)]
SLOTS = 2
MESH = pl.DeviceIdType.MESH
NEG_FILL = -1e30
SCALE = 2.8853900817779268
VMEM = pl.BlockSpec(memory_space=pltpu.VMEM)
SMEM = pl.BlockSpec(memory_space=pltpu.SMEM)
HBM = pl.BlockSpec(memory_space=pltpu.HBM)
VMEM_LIMIT = 40 * 1024 * 1024


def params(**kw):
    return pltpu.CompilerParams(vmem_limit_bytes=VMEM_LIMIT, **kw)


def split3(value):
    high = value.astype(jnp.bfloat16).astype(jnp.float32)
    rest = value - high
    middle = rest.astype(jnp.bfloat16).astype(jnp.float32)
    low = (rest - middle).astype(jnp.bfloat16).astype(jnp.float32)
    return [high, middle, low]


def tile_rows(ref, tiles):
    return jnp.concatenate(
        [ref[pl.ds(q, tiles, stride=CHUNKS), :] for q in range(CHUNKS)], axis=1
    )


def as_columns(pieces):
    rows = sum(piece.shape[0] for piece in pieces)
    pieces = pieces + [jnp.zeros((LANES - rows, TILE), jnp.float32)]
    return jnp.concatenate(pieces, axis=0).T.astype(jnp.bfloat16)


def lane_mask(first, period, which):
    lane = lax.broadcasted_iota(jnp.int32, (1, LANES), 1) - first
    hit = (lane == which) | (lane == which + period) | (lane == which + 2 * period)
    return jnp.where(hit, 1.0, 0.0)


def spread(row):
    return jnp.broadcast_to(row, (TILE, LANES)).astype(jnp.bfloat16)


def tile_at(ref, index):
    return ref[pl.ds(pl.multiple_of(index * TILE, TILE), TILE), :]


def product(left, right):
    return lax.dot_general(
        left, right, (((1,), (1,)), ((), ())), preferred_element_type=jnp.float32
    )


def pair_at(list_ref, live, at):
    return list_ref[jnp.minimum(at, live - 1)]


def pipelined(size, live, fill, drain, add=None):
    groups = lax.div(live + (size - 1), size)

    def step(group, carry):
        if add is not None:
            add(group - 1)
        drain(group)
        fill(group + 1)
        return carry

    if add is None:

        @pl.when(groups > 0)
        def _():
            fill(0)
            lax.fori_loop(0, groups - 1, step, 0)
            drain(groups - 1)

        return

    @pl.when(groups > 1)
    def _():
        fill(0)
        drain(0)
        fill(1)
        lax.fori_loop(1, groups - 1, step, 0)
        add(groups - 2)
        drain(groups - 1)
        add(groups - 1)

    @pl.when(groups == 1)
    def _():
        fill(0)
        drain(0)
        add(0)


def fold_rows(value, op):
    rows, lanes = value.shape
    return op(op(value.reshape(4, rows // 32, 8, lanes), axis=1), axis=0)


def lse_pass(
    list_ref, live, pick, outer_ref, inner_ref, pot_tiles, columns, peak, mass, sums, tops
):
    peak[...] = jnp.full_like(peak, NEG_FILL)
    mass[...] = jnp.zeros_like(mass)
    spare = peak.shape[0] - 1

    def fill(group):
        for u in range(LSE_GROUP):
            outer, inner = pick(pair_at(list_ref, live, group * LSE_GROUP + u))
            left = jnp.concatenate([tile_at(outer_ref, outer), columns[...]], axis=1)
            right = jnp.concatenate(
                [tile_at(inner_ref, inner), spread(lane_mask(0, pot_tiles, outer))], axis=1
            )
            value = product(left, right)
            sums[u] = value
            tops[u] = fold_rows(value, jnp.max)

    def drain(group):
        for u in range(LSE_GROUP):
            at = group * LSE_GROUP + u
            inner = jnp.where(at < live, pick(pair_at(list_ref, live, at))[1], spare)
            before = peak[inner]
            top = jnp.maximum(before, tops[u])
            value = sums[u].reshape(TILE // 8, 8, TILE) - top[None]
            terms = fold_rows(jnp.exp2(value * SCALE).reshape(TILE, TILE), jnp.sum)
            mass[inner] = mass[inner] * jnp.exp2((before - top) * SCALE) + terms
            peak[inner] = top

    pipelined(LSE_GROUP, live, fill, drain)


def lse_finish(peak, mass, out_ref):
    for tile in range(peak.shape[0] - 1):
        top = jnp.max(peak[tile], axis=0, keepdims=True)
        total = jnp.sum(mass[tile] * jnp.exp2((peak[tile] - top) * SCALE), axis=0, keepdims=True)
        lse = jnp.where(total > 0.0, 2.0 * top + jnp.log(total), NEG_FILL)
        for q in range(CHUNKS):
            out_ref[pl.ds(tile * CHUNKS + q, 1), :] = lse[:, q * LANES : (q + 1) * LANES]


def row_kernel(
    cols_hbm,
    counts_hbm,
    g_hbm,
    y_hbm,
    x_hbm,
    lse_ref,
    list_ref,
    rest_ref,
    slot_ref,
    bias_ref,
    x_ref,
    y_ref,
    cols_ref,
    counts_ref,
    g_ref,
    sems,
    columns,
    *sums,
):
    arrivals = [(cols_hbm, cols_ref), (counts_hbm, counts_ref), (g_hbm, g_ref)]
    arrivals += [(y_hbm, y_ref), (x_hbm, x_ref)]
    copies = [
        pltpu.make_async_copy(src, dst, sems.at[i]) for i, (src, dst) in enumerate(arrivals)
    ]
    for copy in copies:
        copy.start()
    row_tiles, most = cols_ref.shape
    col_tiles = y_ref.shape[0] // TILE
    me = lax.axis_index("gy")
    for copy in copies[:3]:
        copy.wait()
    columns[...] = as_columns(split3(tile_rows(g_ref, col_tiles)))
    live, others = jnp.int32(0), jnp.int32(0)
    for row in range(row_tiles):
        count = counts_ref[row]
        base = (row - me) * col_tiles
        first = live
        for slot in range(most):
            pair = cols_ref[row, slot] + base
            owned = (pair >= row * col_tiles) & (pair < (row + 1) * col_tiles) & (slot < count)
            list_ref[live] = pair
            if slot >= SLOTS:
                rest_ref[others] = pair
                others = others + jnp.where(owned & (live - first >= SLOTS), 1, 0)
            live = live + jnp.where(owned, 1, 0)
        for slot in range(SLOTS):
            here = first + slot < live
            pair = list_ref[first + slot]
            slot_ref[row * SLOTS + slot] = jnp.where(here, pair - row * col_tiles, 0)
            bias_ref[row * SLOTS + slot] = jnp.where(here, 0.0, NEG_FILL)
    list_ref[row_tiles * most + SLOTS] = live
    rest_ref[row_tiles * most] = others
    copies[3].wait()
    copies[4].wait()
    pick = lambda pair: (lax.rem(pair, col_tiles), lax.div(pair, col_tiles))
    lse_pass(list_ref, live, pick, y_ref, x_ref, col_tiles, columns, *sums)
    lse_finish(*sums[:2], lse_ref)


def column_kernel(list_ref, x_ref, y_ref, f_ref, lse_ref, columns, *sums):
    row_tiles = x_ref.shape[0] // TILE
    col_tiles = y_ref.shape[0] // TILE
    live = list_ref[list_ref.shape[0] - 1]
    columns[...] = as_columns(split3(tile_rows(f_ref, row_tiles)))
    pick = lambda pair: (lax.div(pair, col_tiles), lax.rem(pair, col_tiles))
    lse_pass(list_ref, live, pick, x_ref, y_ref, row_tiles, columns, *sums)
    lse_finish(*sums[:2], lse_ref)


def bary_potentials(f_ref, g_ref, row_tiles, col_tiles, columns, pots_g, pots_f):
    first = 3 * col_tiles
    pots = split3(tile_rows(g_ref, col_tiles)) + split3(tile_rows(f_ref, row_tiles))
    columns[...] = as_columns(pots)
    lane = lax.broadcasted_iota(jnp.int32, (1, LANES), 1)
    pots_g[...] = columns[...] * spread(jnp.where(lane < first, 1.0, 0.0))
    pots_f[...] = columns[...] * spread(jnp.where(lane < first, 0.0, 1.0)) + spread(
        jnp.where(lane == first + 3 * row_tiles, 1.0, 0.0)
    )


def bary_sums(x_tile, y_tile, pots_g, pots_f, row_mask, col_mask):
    left = jnp.concatenate([y_tile, pots_g[...] + spread(row_mask)], axis=1)
    right = jnp.concatenate([x_tile, pots_f[...] + spread(col_mask)], axis=1)
    return product(left, right)


def weighted(points, weights):
    return lax.dot_general(
        points, weights, (((0,), (0,)), ((), ())), preferred_element_type=jnp.float32
    )


def bary_kernel(
    list_ref,
    x_ref,
    y_ref,
    f_ref,
    g_ref,
    out_ref,
    f_hbm,
    g_hbm,
    columns,
    pots_g,
    pots_f,
    sums,
    rounded,
    sems,
):
    results = [
        pltpu.make_async_copy(f_ref, f_hbm, sems.at[0]),
        pltpu.make_async_copy(g_ref, g_hbm, sems.at[1]),
    ]
    for copy in results:
        copy.start()
    row_tiles = x_ref.shape[0] // TILE
    col_tiles = y_ref.shape[0] // TILE
    width = x_ref.shape[1]
    live = list_ref[list_ref.shape[0] - 1]
    bary_potentials(f_ref, g_ref, row_tiles, col_tiles, columns, pots_g, pots_f)
    out_ref[...] = jnp.zeros_like(out_ref)
    spare = out_ref.shape[0] - 1
    pick = lambda pair: (lax.div(pair, col_tiles), lax.rem(pair, col_tiles))

    def fill(group):
        for u in range(BARY_GROUP):
            row, col = pick(pair_at(list_ref, live, group * BARY_GROUP + u))
            row_mask = lane_mask(3 * col_tiles, row_tiles, row)
            col_mask = lane_mask(0, col_tiles, col)
            x_tile, y_tile = tile_at(x_ref, row), tile_at(y_ref, col)
            sums[u] = bary_sums(x_tile, y_tile, pots_g, pots_f, row_mask, col_mask)

    def drain(group):
        for u in range(BARY_GROUP):
            at = group * BARY_GROUP + u
            row = jnp.where(at < live, pick(pair_at(list_ref, live, at))[0], spare)
            weights = jnp.exp2(sums[u] * SCALE)
            mass = fold_rows(weights, jnp.sum)
            for k, lanes in enumerate(PIECE_LANES):
                out_ref[row, k, width:] += mass[:, lanes]
            rounded[u] = weights.astype(jnp.bfloat16)

    def add(group):
        for u in range(BARY_GROUP):
            at = group * BARY_GROUP + u
            row, col = pick(pair_at(list_ref, live, at))
            row = jnp.where(at < live, row, spare)
            total = weighted(tile_at(y_ref, col), rounded[u])
            for k, lanes in enumerate(PIECE_LANES):
                out_ref[row, k, :width] += total[:, lanes]

    pipelined(BARY_GROUP, live, fill, drain, add)
    for copy in results:
        copy.wait()


def meet(peers):
    barrier = pltpu.get_barrier_semaphore()
    for peer in peers:
        pl.semaphore_signal(barrier, inc=1, device_id=peer, device_id_type=MESH)
    pl.semaphore_wait(barrier, len(peers))


def send(src, dst, send_sem, recv_sem, peer):
    copy = pltpu.make_async_remote_copy(
        src_ref=src,
        dst_ref=dst,
        send_sem=send_sem,
        recv_sem=recv_sem,
        device_id=peer,
        device_id_type=MESH,
    )
    copy.start()
    return copy


def join(parts):
    top = parts[0]
    for part in parts[1:]:
        top = jnp.maximum(top, part)
    total = jnp.exp(parts[0] - top)
    for part in parts[1:]:
        total = total + jnp.exp(part - top)
    return top + jnp.log(total)


def row_join_kernel(n, lse_ref, log_a_ref, f_ref, held, send_sem, recv_sem):
    me = lax.axis_index("gy")
    peers = [{"gy": lax.rem(me + d, n)} for d in range(1, n)]
    meet(peers)
    copies = [
        send(lse_ref, held.at[me], send_sem.at[i], recv_sem.at[i], peer)
        for i, peer in enumerate(peers)
    ]
    held[me] = lse_ref[...]
    for copy in copies:
        copy.wait()
    f_ref[...] = 0.5 * (log_a_ref[...] - join([held[k] for k in range(n)]))


def col_join_kernel(nz, ny, lse_ref, log_b_ref, g_ref, first, part, second, sems):
    me = lax.axis_index("gx")
    z, y = lax.div(me, ny), lax.rem(me, ny)
    y_peers = [{"gx": z * ny + lax.rem(y + d, ny)} for d in range(1, ny)]
    z_peers = [{"gx": lax.rem(z + d, nz) * ny + y} for d in range(1, nz)]
    meet(y_peers + z_peers)
    half = lse_ref.shape[0] // 2
    n = ny
    for stage in range(2):
        held = (first, second)[stage]
        copies = []
        for upper in range(2):
            own = lse_ref.at[pl.ds(upper * half, half)] if stage == 0 else part.at[upper]
            along_y = upper == stage
            at = y if along_y else z
            for i, peer in enumerate(y_peers if along_y else z_peers):
                k = (stage * 2 + upper) * (n - 1) + i
                copies.append(send(own, held.at[upper, at], sems.at[0, k], sems.at[1, k], peer))
            held[upper, at] = own[...]
        for copy in copies:
            copy.wait()
        for upper in range(2):
            joined = join([held[upper, k] for k in range(n)])
            if stage == 0:
                part[upper] = joined
            else:
                rows = slice(upper * half, (upper + 1) * half)
                g_ref[rows] = 0.5 * (log_b_ref[rows] - joined)


def bary_join_kernel(
    n,
    slot_ref,
    bias_ref,
    x_ref,
    y_ref,
    f_ref,
    g_ref,
    part_ref,
    out_ref,
    columns,
    pots_g,
    pots_f,
    masks,
    sums,
    rounded,
    whole,
    near,
    relay,
    left_in,
    right_in,
    sems,
):
    me = lax.axis_index("gy")
    chips = n // 2
    chip, core = lax.div(me, 2), lax.rem(me, 2)
    other = 1 - core
    width = out_ref.shape[1]
    row_tiles, col_tiles = x_ref.shape[0] // TILE, y_ref.shape[0]
    split = width // 2
    low, high = slice(0, split), slice(split, width + 8)
    places = [lax.rem(chip + d, chips) for d in range(chips)]
    sibling = {"gy": chip * 2 + other}
    right, left = {"gy": places[1] * 2 + core}, {"gy": places[3] * 2 + core}
    barrier = pltpu.get_barrier_semaphore()
    for peer in (sibling, right, left):
        pl.semaphore_signal(barrier, inc=1, device_id=peer, device_id_type=MESH)
    bary_potentials(f_ref, g_ref, row_tiles, col_tiles, columns, pots_g, pots_f)

    lane = lax.broadcasted_iota(jnp.int32, (1, LANES), 1)
    bias_lane = jnp.where(lane == 3 * (col_tiles + row_tiles), 1.0, 0.0)
    for col in range(col_tiles):
        masks[col] = lane_mask(0, col_tiles, col)

    def take(rows):
        cols = []
        for i, row in enumerate(rows):
            row_mask = lane_mask(3 * col_tiles, row_tiles, row)
            for k in range(SLOTS):
                col = slot_ref[row * SLOTS + k]
                cols.append(col)
                sums[i * SLOTS + k] = bary_sums(
                    tile_at(x_ref, row),
                    y_ref[col],
                    pots_g,
                    pots_f,
                    row_mask + bias_lane * bias_ref[row * SLOTS + k],
                    masks[col],
                )
        for i, row in enumerate(rows):
            mass = 0.0
            for k in range(i * SLOTS, (i + 1) * SLOTS):
                weights = jnp.exp2(sums[k] * SCALE)
                mass = mass + fold_rows(weights, jnp.sum)
                rounded[k] = weights.astype(jnp.bfloat16)
            for k, lanes in enumerate(PIECE_LANES):
                whole[row, k, width:] = part_ref[row, k, width:] + mass[:, lanes]
        for i, row in enumerate(rows):
            total = 0.0
            for k in range(i * SLOTS, (i + 1) * SLOTS):
                total = total + weighted(y_ref[cols[k]], rounded[k])
            for k, lanes in enumerate(PIECE_LANES):
                whole[row, k, :width] = part_ref[row, k, :width] + total[:, lanes]

    used = [0]

    def go(src, dst, peer):
        k = used[0]
        used[0] += 1
        return send(src, dst, sems.at[0, k], sems.at[1, k], peer)

    def tile(d, kind):
        return places[d] * 2 + kind

    pieces = list(range(PIECES))
    inside, waits = {}, []

    def give_inside(d):
        inside[d] = go(whole.at[tile(d, other)], near.at[d], sibling)

    def add_inside(d):
        inside[d].wait()
        near[d] = near[d] + whole[tile(d, core)]

    take([tile(2, other)])
    pl.semaphore_wait(barrier, 3)
    give_inside(2)
    take([tile(2, core)])
    add_inside(2)
    far = []
    for piece in pieces:
        far.append(
            (
                go(near.at[2, piece, low], relay.at[piece, low], right),
                go(near.at[2, piece, high], relay.at[piece, high], left),
            )
        )
    take([tile(1, other), tile(3, other)])
    give_inside(1)
    give_inside(3)
    take([tile(1, core), tile(3, core)])
    add_inside(1)
    add_inside(3)
    direct, passed = [], []

    def give_direct(piece):
        direct.append(
            (
                go(near.at[1, piece, high], left_in.at[piece, high], right),
                go(near.at[3, piece, low], right_in.at[piece, low], left),
            )
        )

    for piece in pieces[:2]:
        give_direct(piece)
    take([tile(0, other), tile(0, core)])
    give_inside(0)
    for k, piece in enumerate(pieces):
        far[k][0].wait()
        near[1, piece, low] = near[1, piece, low] + relay[piece, low]
        to_right = go(near.at[1, piece, low], left_in.at[piece, low], right)
        far[k][1].wait()
        near[3, piece, high] = near[3, piece, high] + relay[piece, high]
        to_left = go(near.at[3, piece, high], right_in.at[piece, high], left)
        passed.append((to_right, to_left))
        for ahead in pieces[k + 2 : k + 3]:
            give_direct(ahead)
    add_inside(0)

    def rows_of(place, kind, first, count):
        start = (place * 2 + kind) * TILE + first
        return out_ref.at[pl.ds(pl.multiple_of(start, 8), count)]

    size = TILE // PIECES
    own = []
    for k, piece in enumerate(pieces):
        for copy in direct[k] + passed[k]:
            copy.wait()
        total = near[0, k] + left_in[k] + right_in[k]
        ratio = total[:width] / jnp.sum(total[width:], axis=0, keepdims=True)
        mine = rows_of(chip, core, k * size, size)
        mine[...] = ratio.T
        own.append((go(mine, mine, right), go(mine, mine, left)))
        waits.append(go(mine, mine, sibling))
    onward = []
    for k in range(PIECES):
        for side in range(2):
            own[k][side].wait()
            place = places[3] if side == 0 else places[1]
            block = rows_of(place, core, k * size + side * size // 2, size // 2)
            onward.append((k, side, go(block, block, right if side == 0 else left)))
            block = rows_of(place, core, k * size, size)
            waits.append(go(block, block, sibling))
    for k, side, copy in onward:
        copy.wait()
        block = rows_of(places[2], core, k * size + side * size // 2, size // 2)
        waits.append(go(block, block, sibling))
    for copy in waits:
        copy.wait()


def local(gx_size, gy_size, points_x, points_y, g_init, log_a, log_b, tile_cols, tile_counts):
    row_tiles, most = tile_cols.shape
    rows, width = points_x.shape
    cols = points_y.shape[0]
    col_tiles = cols // TILE
    nz = 1
    while nz * nz < gx_size:
        nz *= 2
    ny = gx_size // nz
    f32, i32, bf16 = jnp.float32, jnp.int32, jnp.bfloat16
    row_shape, col_shape = (rows // LANES, LANES), (cols // LANES, LANES)
    dma = pltpu.SemaphoreType.DMA

    def lse_scratch(tiles):
        return [
            pltpu.VMEM((TILE, LANES), bf16),
            pltpu.VMEM((tiles + 1, 8, TILE), f32),
            pltpu.VMEM((tiles + 1, 8, TILE), f32),
            pltpu.VMEM((LSE_GROUP, TILE, TILE), f32),
            pltpu.VMEM((LSE_GROUP, 8, TILE), f32),
        ]

    sources = (tile_cols, tile_counts, g_init.reshape(col_shape), points_y, points_x)
    row_lse, pairs, rest, slots, biases, points_x, points_y = pl.pallas_call(
        row_kernel,
        out_shape=(
            pltpu.VMEM(row_shape, f32),
            jax.ShapeDtypeStruct((row_tiles * most + SLOTS + 1,), i32),
            jax.ShapeDtypeStruct((row_tiles * most + 1,), i32),
            jax.ShapeDtypeStruct((row_tiles * SLOTS,), i32),
            jax.ShapeDtypeStruct((row_tiles * SLOTS,), f32),
            pltpu.VMEM(points_x.shape, bf16),
            pltpu.VMEM(points_y.shape, bf16),
        ),
        in_specs=[HBM] * 5,
        out_specs=(VMEM, SMEM, SMEM, SMEM, SMEM, VMEM, VMEM),
        scratch_shapes=[
            pltpu.SMEM(tile_cols.shape, i32),
            pltpu.SMEM(tile_counts.shape, i32),
            pltpu.VMEM(col_shape, f32),
            dma((5,)),
        ]
        + lse_scratch(row_tiles),
        compiler_params=params(),
        name="row_pass",
    )(*[pltpu.with_memory_space_constraint(source, pltpu.HBM) for source in sources])

    f_pot = pl.pallas_call(
        functools.partial(row_join_kernel, gy_size),
        out_shape=jax.ShapeDtypeStruct(row_shape, f32),
        in_specs=[VMEM, VMEM],
        out_specs=VMEM,
        scratch_shapes=[
            pltpu.VMEM((gy_size,) + row_shape, f32),
            dma((gy_size - 1,)),
            dma((gy_size - 1,)),
        ],
        compiler_params=params(collective_id=0, has_side_effects=True),
        name="row_join",
    )(row_lse, log_a.reshape(row_shape))

    col_lse = pl.pallas_call(
        column_kernel,
        out_shape=jax.ShapeDtypeStruct(col_shape, f32),
        in_specs=[SMEM, VMEM, VMEM, VMEM],
        out_specs=VMEM,
        scratch_shapes=lse_scratch(col_tiles),
        compiler_params=params(),
        name="column_pass",
    )(pairs, points_x, points_y, f_pot)

    half = (2, col_shape[0] // 2, LANES)
    g_pot = pl.pallas_call(
        functools.partial(col_join_kernel, nz, ny),
        out_shape=jax.ShapeDtypeStruct(col_shape, f32),
        in_specs=[VMEM, VMEM],
        out_specs=VMEM,
        scratch_shapes=[
            pltpu.VMEM((2, ny) + half[1:], f32),
            pltpu.VMEM(half, f32),
            pltpu.VMEM((2, ny) + half[1:], f32),
            dma((2, 4 * (ny - 1))),
        ],
        compiler_params=params(collective_id=1, has_side_effects=True),
        name="column_join",
    )(col_lse, log_b.reshape(col_shape))

    partial, f_out, g_out = pl.pallas_call(
        bary_kernel,
        out_shape=(
            jax.ShapeDtypeStruct((row_tiles + 1, PIECES, width + 8, PIECE), f32),
            jax.ShapeDtypeStruct(row_shape, f32),
            jax.ShapeDtypeStruct(col_shape, f32),
        ),
        in_specs=[SMEM, VMEM, VMEM, VMEM, VMEM],
        out_specs=(VMEM, HBM, HBM),
        scratch_shapes=[pltpu.VMEM((TILE, LANES), bf16)] * 3
        + [
            pltpu.VMEM((BARY_GROUP, TILE, TILE), f32),
            pltpu.VMEM((BARY_GROUP, TILE, TILE), bf16),
            dma((2,)),
        ],
        compiler_params=params(),
        name="bary_pass",
    )(rest, points_x, points_y, f_pot, g_pot)

    barycenter = pl.pallas_call(
        functools.partial(bary_join_kernel, gy_size),
        out_shape=jax.ShapeDtypeStruct((rows, width), f32),
        in_specs=[SMEM] * 2 + [VMEM] * 5,
        out_specs=VMEM,
        scratch_shapes=[pltpu.VMEM((TILE, LANES), bf16)] * 3
        + [
            pltpu.VMEM((col_tiles, 1, LANES), f32),
            pltpu.VMEM((2 * SLOTS, TILE, TILE), f32),
            pltpu.VMEM((2 * SLOTS, TILE, TILE), bf16),
            pltpu.VMEM((row_tiles, PIECES, width + 8, PIECE), f32),
            pltpu.VMEM((4, PIECES, width + 8, PIECE), f32),
        ]
        + [pltpu.VMEM((PIECES, width + 8, PIECE), f32)] * 3
        + [dma((2, 4 + 15 * PIECES))],
        compiler_params=params(collective_id=2, has_side_effects=True),
        name="bary_join",
    )(slots, biases, points_x, points_y.reshape(col_tiles, TILE, width), f_pot, g_pot, partial)
    return (f_out.reshape(-1), g_out.reshape(-1), barycenter)


def solution(mesh):
    in_specs = (P("gx", None), P("gy", None), P("gy"), P("gx"), P("gy"), P("gx", None), P("gx"))
    out_specs = (P("gx"), P("gy"), P("gx", None))
    body = functools.partial(local, mesh.shape["gx"], mesh.shape["gy"])
    return jax.shard_map(body, mesh=mesh, in_specs=in_specs, out_specs=out_specs, check_vma=False)
```

```python
import functools

import jax
import jax.numpy as jnp
from jax import lax
from jax.experimental import pallas as pl
from jax.experimental.pallas import tpu as pltpu
from jax.sharding import PartitionSpec as P

TILE = 512
LANES = 128
CHUNKS = TILE // LANES
LSE_GROUP = 2
BARY_GROUP = 2
PIECES = 4
PIECE = TILE // PIECES
PIECE_LANES = [slice(k * PIECE, (k + 1) * PIECE) for k in range(PIECES)]
SLOTS = 2
MESH = pl.DeviceIdType.MESH
NEG_FILL = -1e30
SCALE = 2.8853900817779268
VMEM = pl.BlockSpec(memory_space=pltpu.VMEM)
SMEM = pl.BlockSpec(memory_space=pltpu.SMEM)
HBM = pl.BlockSpec(memory_space=pltpu.HBM)
ANY = pl.BlockSpec(memory_space=pl.ANY)
VMEM_LIMIT = 40 * 1024 * 1024


def params(**kw):
    return pltpu.CompilerParams(vmem_limit_bytes=VMEM_LIMIT, **kw)


def split3(value):
    high = value.astype(jnp.bfloat16).astype(jnp.float32)
    rest = value - high
    middle = rest.astype(jnp.bfloat16).astype(jnp.float32)
    low = (rest - middle).astype(jnp.bfloat16).astype(jnp.float32)
    return [high, middle, low]


def tile_rows(ref, tiles):
    return jnp.concatenate(
        [ref[pl.ds(q, tiles, stride=CHUNKS), :] for q in range(CHUNKS)], axis=1
    )


def as_columns(pieces):
    rows = sum(piece.shape[0] for piece in pieces)
    pieces = pieces + [jnp.zeros((LANES - rows, TILE), jnp.float32)]
    return jnp.concatenate(pieces, axis=0).T.astype(jnp.bfloat16)


def lane_mask(first, period, which):
    lane = lax.broadcasted_iota(jnp.int32, (1, LANES), 1) - first
    hit = (lane == which) | (lane == which + period) | (lane == which + 2 * period)
    return jnp.where(hit, 1.0, 0.0)


def spread(row):
    return jnp.broadcast_to(row, (TILE, LANES)).astype(jnp.bfloat16)


def tile_at(ref, index):
    return ref[pl.ds(pl.multiple_of(index * TILE, TILE), TILE), :]


def product(left, right):
    return lax.dot_general(
        left, right, (((1,), (1,)), ((), ())), preferred_element_type=jnp.float32
    )


def pair_at(list_ref, live, at):
    return list_ref[jnp.minimum(at, live - 1)]


def pipelined(size, live, fill, drain, add=None):
    groups = lax.div(live + (size - 1), size)

    def step(group, carry):
        if add is not None:
            add(group - 1)
        drain(group)
        fill(group + 1)
        return carry

    if add is None:

        @pl.when(groups > 0)
        def _():
            fill(0)
            lax.fori_loop(0, groups - 1, step, 0)
            drain(groups - 1)

        return

    @pl.when(groups > 1)
    def _():
        fill(0)
        drain(0)
        fill(1)
        lax.fori_loop(1, groups - 1, step, 0)
        add(groups - 2)
        drain(groups - 1)
        add(groups - 1)

    @pl.when(groups == 1)
    def _():
        fill(0)
        drain(0)
        add(0)


def fold_rows(value, op):
    rows, lanes = value.shape
    return op(op(value.reshape(4, rows // 32, 8, lanes), axis=1), axis=0)


def lse_pass(
    list_ref, live, pick, outer_ref, inner_ref, pot_tiles, columns, peak, mass, sums, tops
):
    peak[...] = jnp.full_like(peak, NEG_FILL)
    mass[...] = jnp.zeros_like(mass)
    spare = peak.shape[0] - 1

    def fill(group):
        for u in range(LSE_GROUP):
            outer, inner = pick(pair_at(list_ref, live, group * LSE_GROUP + u))
            left = jnp.concatenate([tile_at(outer_ref, outer), columns[...]], axis=1)
            right = jnp.concatenate(
                [tile_at(inner_ref, inner), spread(lane_mask(0, pot_tiles, outer))], axis=1
            )
            value = product(left, right)
            sums[u] = value
            tops[u] = fold_rows(value, jnp.max)

    def drain(group):
        for u in range(LSE_GROUP):
            at = group * LSE_GROUP + u
            inner = jnp.where(at < live, pick(pair_at(list_ref, live, at))[1], spare)
            before = peak[inner]
            top = jnp.maximum(before, tops[u])
            value = sums[u].reshape(TILE // 8, 8, TILE) - top[None]
            terms = fold_rows(jnp.exp2(value * SCALE).reshape(TILE, TILE), jnp.sum)
            mass[inner] = mass[inner] * jnp.exp2((before - top) * SCALE) + terms
            peak[inner] = top

    pipelined(LSE_GROUP, live, fill, drain)


def lse_finish(peak, mass, out_ref):
    for tile in range(peak.shape[0] - 1):
        top = jnp.max(peak[tile], axis=0, keepdims=True)
        total = jnp.sum(mass[tile] * jnp.exp2((peak[tile] - top) * SCALE), axis=0, keepdims=True)
        lse = jnp.where(total > 0.0, 2.0 * top + jnp.log(total), NEG_FILL)
        for q in range(CHUNKS):
            out_ref[pl.ds(tile * CHUNKS + q, 1), :] = lse[:, q * LANES : (q + 1) * LANES]


def row_kernel(
    cols_hbm,
    counts_hbm,
    g_hbm,
    y_hbm,
    x_hbm,
    lse_ref,
    list_any,
    rest_any,
    slot_any,
    bias_any,
    x_ref,
    y_ref,
    list_ref,
    rest_ref,
    slot_ref,
    bias_ref,
    cols_ref,
    counts_ref,
    g_ref,
    sems,
    columns,
    *sums,
):
    arrivals = [(cols_hbm, cols_ref), (counts_hbm, counts_ref), (g_hbm, g_ref)]
    arrivals += [(y_hbm, y_ref), (x_hbm, x_ref)]
    copies = [
        pltpu.make_async_copy(src, dst, sems.at[i]) for i, (src, dst) in enumerate(arrivals)
    ]
    for copy in copies:
        copy.start()
    row_tiles, most = cols_ref.shape
    col_tiles = y_ref.shape[0] // TILE
    me = lax.axis_index("gy")
    for copy in copies[:3]:
        copy.wait()
    columns[...] = as_columns(split3(tile_rows(g_ref, col_tiles)))
    live, others = jnp.int32(0), jnp.int32(0)
    for row in range(row_tiles):
        count = counts_ref[row]
        base = (row - me) * col_tiles
        first = live
        for slot in range(most):
            pair = cols_ref[row, slot] + base
            owned = (pair >= row * col_tiles) & (pair < (row + 1) * col_tiles) & (slot < count)
            list_ref[live] = pair
            if slot >= SLOTS:
                rest_ref[others] = pair
                others = others + jnp.where(owned & (live - first >= SLOTS), 1, 0)
            live = live + jnp.where(owned, 1, 0)
        for slot in range(SLOTS):
            here = first + slot < live
            pair = list_ref[first + slot]
            slot_ref[row * SLOTS + slot] = jnp.where(here, pair - row * col_tiles, 0)
            bias_ref[row * SLOTS + slot] = jnp.where(here, 0.0, NEG_FILL)
    list_ref[row_tiles * most + SLOTS] = live
    rest_ref[row_tiles * most] = others
    leaving = [(list_ref, list_any), (rest_ref, rest_any), (slot_ref, slot_any)]
    leaving += [(bias_ref, bias_any)]
    leaving = [
        pltpu.make_async_copy(src, dst, sems.at[5 + i]) for i, (src, dst) in enumerate(leaving)
    ]
    for copy in leaving:
        copy.start()
    copies[3].wait()
    copies[4].wait()
    pick = lambda pair: (lax.rem(pair, col_tiles), lax.div(pair, col_tiles))
    lse_pass(list_ref, live, pick, y_ref, x_ref, col_tiles, columns, *sums)
    lse_finish(*sums[:2], lse_ref)
    for copy in leaving:
        copy.wait()


def column_kernel(list_any, x_ref, y_ref, f_ref, lse_ref, list_ref, sem, columns, *sums):
    fetch = pltpu.make_async_copy(list_any, list_ref, sem)
    fetch.start()
    row_tiles = x_ref.shape[0] // TILE
    col_tiles = y_ref.shape[0] // TILE
    columns[...] = as_columns(split3(tile_rows(f_ref, row_tiles)))
    fetch.wait()
    live = list_ref[list_ref.shape[0] - 1]
    pick = lambda pair: (lax.div(pair, col_tiles), lax.rem(pair, col_tiles))
    lse_pass(list_ref, live, pick, x_ref, y_ref, row_tiles, columns, *sums)
    lse_finish(*sums[:2], lse_ref)


def bary_potentials(f_ref, g_ref, row_tiles, col_tiles, columns, pots_g, pots_f):
    first = 3 * col_tiles
    pots = split3(tile_rows(g_ref, col_tiles)) + split3(tile_rows(f_ref, row_tiles))
    columns[...] = as_columns(pots)
    lane = lax.broadcasted_iota(jnp.int32, (1, LANES), 1)
    pots_g[...] = columns[...] * spread(jnp.where(lane < first, 1.0, 0.0))
    pots_f[...] = columns[...] * spread(jnp.where(lane < first, 0.0, 1.0)) + spread(
        jnp.where(lane == first + 3 * row_tiles, 1.0, 0.0)
    )


def bary_sums(x_tile, y_tile, pots_g, pots_f, row_mask, col_mask):
    left = jnp.concatenate([y_tile, pots_g[...] + spread(row_mask)], axis=1)
    right = jnp.concatenate([x_tile, pots_f[...] + spread(col_mask)], axis=1)
    return product(left, right)


def weighted(points, weights):
    return lax.dot_general(
        points, weights, (((0,), (0,)), ((), ())), preferred_element_type=jnp.float32
    )


def bary_kernel(
    list_any,
    x_ref,
    y_ref,
    f_ref,
    g_ref,
    out_ref,
    f_hbm,
    g_hbm,
    list_ref,
    columns,
    pots_g,
    pots_f,
    sums,
    rounded,
    sems,
):
    fetch = pltpu.make_async_copy(list_any, list_ref, sems.at[2])
    fetch.start()
    results = [
        pltpu.make_async_copy(f_ref, f_hbm, sems.at[0]),
        pltpu.make_async_copy(g_ref, g_hbm, sems.at[1]),
    ]
    for copy in results:
        copy.start()
    row_tiles = x_ref.shape[0] // TILE
    col_tiles = y_ref.shape[0] // TILE
    width = x_ref.shape[1]
    bary_potentials(f_ref, g_ref, row_tiles, col_tiles, columns, pots_g, pots_f)
    out_ref[...] = jnp.zeros_like(out_ref)
    fetch.wait()
    live = list_ref[list_ref.shape[0] - 1]
    spare = out_ref.shape[0] - 1
    pick = lambda pair: (lax.div(pair, col_tiles), lax.rem(pair, col_tiles))

    def fill(group):
        for u in range(BARY_GROUP):
            row, col = pick(pair_at(list_ref, live, group * BARY_GROUP + u))
            row_mask = lane_mask(3 * col_tiles, row_tiles, row)
            col_mask = lane_mask(0, col_tiles, col)
            x_tile, y_tile = tile_at(x_ref, row), tile_at(y_ref, col)
            sums[u] = bary_sums(x_tile, y_tile, pots_g, pots_f, row_mask, col_mask)

    def drain(group):
        for u in range(BARY_GROUP):
            at = group * BARY_GROUP + u
            row = jnp.where(at < live, pick(pair_at(list_ref, live, at))[0], spare)
            weights = jnp.exp2(sums[u] * SCALE)
            mass = fold_rows(weights, jnp.sum)
            for k, lanes in enumerate(PIECE_LANES):
                out_ref[row, k, width:] += mass[:, lanes]
            rounded[u] = weights.astype(jnp.bfloat16)

    def add(group):
        for u in range(BARY_GROUP):
            at = group * BARY_GROUP + u
            row, col = pick(pair_at(list_ref, live, at))
            row = jnp.where(at < live, row, spare)
            total = weighted(tile_at(y_ref, col), rounded[u])
            for k, lanes in enumerate(PIECE_LANES):
                out_ref[row, k, :width] += total[:, lanes]

    pipelined(BARY_GROUP, live, fill, drain, add)
    for copy in results:
        copy.wait()


def meet(peers):
    barrier = pltpu.get_barrier_semaphore()
    for peer in peers:
        pl.semaphore_signal(barrier, inc=1, device_id=peer, device_id_type=MESH)
    pl.semaphore_wait(barrier, len(peers))


def send(src, dst, send_sem, recv_sem, peer):
    copy = pltpu.make_async_remote_copy(
        src_ref=src,
        dst_ref=dst,
        send_sem=send_sem,
        recv_sem=recv_sem,
        device_id=peer,
        device_id_type=MESH,
    )
    copy.start()
    return copy


def join(parts):
    top = parts[0]
    for part in parts[1:]:
        top = jnp.maximum(top, part)
    total = jnp.exp(parts[0] - top)
    for part in parts[1:]:
        total = total + jnp.exp(part - top)
    return top + jnp.log(total)


def row_join_kernel(n, lse_ref, log_a_ref, f_ref, held, send_sem, recv_sem):
    me = lax.axis_index("gy")
    peers = [{"gy": lax.rem(me + d, n)} for d in range(1, n)]
    meet(peers)
    copies = [
        send(lse_ref, held.at[me], send_sem.at[i], recv_sem.at[i], peer)
        for i, peer in enumerate(peers)
    ]
    held[me] = lse_ref[...]
    for copy in copies:
        copy.wait()
    f_ref[...] = 0.5 * (log_a_ref[...] - join([held[k] for k in range(n)]))


def col_join_kernel(nz, ny, lse_ref, log_b_ref, g_ref, first, part, second, sems):
    me = lax.axis_index("gx")
    z, y = lax.div(me, ny), lax.rem(me, ny)
    y_peers = [{"gx": z * ny + lax.rem(y + d, ny)} for d in range(1, ny)]
    z_peers = [{"gx": lax.rem(z + d, nz) * ny + y} for d in range(1, nz)]
    meet(y_peers + z_peers)
    half = lse_ref.shape[0] // 2
    n = ny
    for stage in range(2):
        held = (first, second)[stage]
        copies = []
        for upper in range(2):
            own = lse_ref.at[pl.ds(upper * half, half)] if stage == 0 else part.at[upper]
            along_y = upper == stage
            at = y if along_y else z
            for i, peer in enumerate(y_peers if along_y else z_peers):
                k = (stage * 2 + upper) * (n - 1) + i
                copies.append(send(own, held.at[upper, at], sems.at[0, k], sems.at[1, k], peer))
            held[upper, at] = own[...]
        for copy in copies:
            copy.wait()
        for upper in range(2):
            joined = join([held[upper, k] for k in range(n)])
            if stage == 0:
                part[upper] = joined
            else:
                rows = slice(upper * half, (upper + 1) * half)
                g_ref[rows] = 0.5 * (log_b_ref[rows] - joined)


def bary_join_kernel(
    n,
    slot_any,
    bias_any,
    x_ref,
    y_ref,
    f_ref,
    g_ref,
    part_ref,
    out_ref,
    slot_ref,
    bias_ref,
    here,
    columns,
    pots_g,
    pots_f,
    masks,
    sums,
    rounded,
    whole,
    near,
    relay,
    left_in,
    right_in,
    sems,
):
    me = lax.axis_index("gy")
    chips = n // 2
    chip, core = lax.div(me, 2), lax.rem(me, 2)
    other = 1 - core
    width = out_ref.shape[1]
    row_tiles, col_tiles = x_ref.shape[0] // TILE, y_ref.shape[0]
    split = width // 2
    low, high = slice(0, split), slice(split, width + 8)
    places = [lax.rem(chip + d, chips) for d in range(chips)]
    sibling = {"gy": chip * 2 + other}
    right, left = {"gy": places[1] * 2 + core}, {"gy": places[3] * 2 + core}
    barrier = pltpu.get_barrier_semaphore()
    for peer in (sibling, right, left):
        pl.semaphore_signal(barrier, inc=1, device_id=peer, device_id_type=MESH)
    fetches = [
        pltpu.make_async_copy(slot_any, slot_ref, here.at[0]),
        pltpu.make_async_copy(bias_any, bias_ref, here.at[1]),
    ]
    for fetch in fetches:
        fetch.start()
    bary_potentials(f_ref, g_ref, row_tiles, col_tiles, columns, pots_g, pots_f)
    lane = lax.broadcasted_iota(jnp.int32, (1, LANES), 1)
    bias_lane = jnp.where(lane == 3 * (col_tiles + row_tiles), 1.0, 0.0)
    for col in range(col_tiles):
        masks[col] = lane_mask(0, col_tiles, col)
    for fetch in fetches:
        fetch.wait()

    def take(rows):
        cols = []
        for i, row in enumerate(rows):
            row_mask = lane_mask(3 * col_tiles, row_tiles, row)
            for k in range(SLOTS):
                col = slot_ref[row * SLOTS + k]
                cols.append(col)
                sums[i * SLOTS + k] = bary_sums(
                    tile_at(x_ref, row),
                    y_ref[col],
                    pots_g,
                    pots_f,
                    row_mask + bias_lane * bias_ref[row * SLOTS + k],
                    masks[col],
                )
        for i, row in enumerate(rows):
            mass = 0.0
            for k in range(i * SLOTS, (i + 1) * SLOTS):
                weights = jnp.exp2(sums[k] * SCALE)
                mass = mass + fold_rows(weights, jnp.sum)
                rounded[k] = weights.astype(jnp.bfloat16)
            for k, lanes in enumerate(PIECE_LANES):
                whole[row, k, width:] = part_ref[row, k, width:] + mass[:, lanes]
        for i, row in enumerate(rows):
            total = 0.0
            for k in range(i * SLOTS, (i + 1) * SLOTS):
                total = total + weighted(y_ref[cols[k]], rounded[k])
            for k, lanes in enumerate(PIECE_LANES):
                whole[row, k, :width] = part_ref[row, k, :width] + total[:, lanes]

    used = [0]

    def go(src, dst, peer):
        k = used[0]
        used[0] += 1
        return send(src, dst, sems.at[0, k], sems.at[1, k], peer)

    def tile(d, kind):
        return places[d] * 2 + kind

    pieces = list(range(PIECES))
    inside, waits = {}, []

    def give_inside(d):
        inside[d] = go(whole.at[tile(d, other)], near.at[d], sibling)

    def add_inside(d):
        inside[d].wait()
        near[d] = near[d] + whole[tile(d, core)]

    take([tile(2, other)])
    pl.semaphore_wait(barrier, 3)
    give_inside(2)
    take([tile(2, core)])
    add_inside(2)
    far = []
    for piece in pieces:
        far.append(
            (
                go(near.at[2, piece, low], relay.at[piece, low], right),
                go(near.at[2, piece, high], relay.at[piece, high], left),
            )
        )
    take([tile(1, other), tile(3, other)])
    give_inside(1)
    give_inside(3)
    take([tile(1, core), tile(3, core)])
    add_inside(1)
    add_inside(3)
    direct, passed = [], []

    def give_direct(piece):
        direct.append(
            (
                go(near.at[1, piece, high], left_in.at[piece, high], right),
                go(near.at[3, piece, low], right_in.at[piece, low], left),
            )
        )

    for piece in pieces[:2]:
        give_direct(piece)
    take([tile(0, other), tile(0, core)])
    give_inside(0)
    for k, piece in enumerate(pieces):
        far[k][0].wait()
        near[1, piece, low] = near[1, piece, low] + relay[piece, low]
        to_right = go(near.at[1, piece, low], left_in.at[piece, low], right)
        far[k][1].wait()
        near[3, piece, high] = near[3, piece, high] + relay[piece, high]
        to_left = go(near.at[3, piece, high], right_in.at[piece, high], left)
        passed.append((to_right, to_left))
        for ahead in pieces[k + 2 : k + 3]:
            give_direct(ahead)
    add_inside(0)

    def rows_of(place, kind, first, count):
        start = (place * 2 + kind) * TILE + first
        return out_ref.at[pl.ds(pl.multiple_of(start, 8), count)]

    size = TILE // PIECES
    own = []
    for k, piece in enumerate(pieces):
        for copy in direct[k] + passed[k]:
            copy.wait()
        total = near[0, k] + left_in[k] + right_in[k]
        ratio = total[:width] / jnp.sum(total[width:], axis=0, keepdims=True)
        mine = rows_of(chip, core, k * size, size)
        mine[...] = ratio.T
        own.append((go(mine, mine, right), go(mine, mine, left)))
        waits.append(go(mine, mine, sibling))
    onward = []
    for k in range(PIECES):
        for side in range(2):
            own[k][side].wait()
            place = places[3] if side == 0 else places[1]
            block = rows_of(place, core, k * size + side * size // 2, size // 2)
            onward.append((k, side, go(block, block, right if side == 0 else left)))
            block = rows_of(place, core, k * size, size)
            waits.append(go(block, block, sibling))
    for k, side, copy in onward:
        copy.wait()
        block = rows_of(places[2], core, k * size + side * size // 2, size // 2)
        waits.append(go(block, block, sibling))
    for copy in waits:
        copy.wait()


def local(gx_size, gy_size, points_x, points_y, g_init, log_a, log_b, tile_cols, tile_counts):
    row_tiles, most = tile_cols.shape
    rows, width = points_x.shape
    cols = points_y.shape[0]
    col_tiles = cols // TILE
    nz = 1
    while nz * nz < gx_size:
        nz *= 2
    ny = gx_size // nz
    f32, i32, bf16 = jnp.float32, jnp.int32, jnp.bfloat16
    row_shape, col_shape = (rows // LANES, LANES), (cols // LANES, LANES)
    dma = pltpu.SemaphoreType.DMA

    def lse_scratch(tiles):
        return [
            pltpu.VMEM((TILE, LANES), bf16),
            pltpu.VMEM((tiles + 1, 8, TILE), f32),
            pltpu.VMEM((tiles + 1, 8, TILE), f32),
            pltpu.VMEM((LSE_GROUP, TILE, TILE), f32),
            pltpu.VMEM((LSE_GROUP, 8, TILE), f32),
        ]

    sources = (tile_cols, tile_counts, g_init.reshape(col_shape), points_y, points_x)
    lists = (
        ((row_tiles * most + SLOTS + 1,), i32),
        ((row_tiles * most + 1,), i32),
        ((row_tiles * SLOTS,), i32),
        ((row_tiles * SLOTS,), f32),
    )
    row_lse, pairs, rest, slots, biases, points_x, points_y = pl.pallas_call(
        row_kernel,
        out_shape=(
            pltpu.VMEM(row_shape, f32),
            *[jax.ShapeDtypeStruct(*a) for a in lists],
            pltpu.VMEM(points_x.shape, bf16),
            pltpu.VMEM(points_y.shape, bf16),
        ),
        in_specs=[HBM] * 5,
        out_specs=(VMEM, ANY, ANY, ANY, ANY, VMEM, VMEM),
        scratch_shapes=[pltpu.SMEM(*a) for a in lists]
        + [
            pltpu.SMEM(tile_cols.shape, i32),
            pltpu.SMEM(tile_counts.shape, i32),
            pltpu.VMEM(col_shape, f32),
            dma((9,)),
        ]
        + lse_scratch(row_tiles),
        compiler_params=params(),
        name="row_pass",
    )(*[pltpu.with_memory_space_constraint(source, pltpu.HBM) for source in sources])

    f_pot = pl.pallas_call(
        functools.partial(row_join_kernel, gy_size),
        out_shape=jax.ShapeDtypeStruct(row_shape, f32),
        in_specs=[VMEM, VMEM],
        out_specs=VMEM,
        scratch_shapes=[
            pltpu.VMEM((gy_size,) + row_shape, f32),
            dma((gy_size - 1,)),
            dma((gy_size - 1,)),
        ],
        compiler_params=params(collective_id=0, has_side_effects=True),
        name="row_join",
    )(row_lse, log_a.reshape(row_shape))

    col_lse = pl.pallas_call(
        column_kernel,
        out_shape=jax.ShapeDtypeStruct(col_shape, f32),
        in_specs=[ANY, VMEM, VMEM, VMEM],
        out_specs=VMEM,
        scratch_shapes=[pltpu.SMEM(pairs.shape, i32), dma] + lse_scratch(col_tiles),
        compiler_params=params(),
        name="column_pass",
    )(pairs, points_x, points_y, f_pot)

    half = (2, col_shape[0] // 2, LANES)
    g_pot = pl.pallas_call(
        functools.partial(col_join_kernel, nz, ny),
        out_shape=jax.ShapeDtypeStruct(col_shape, f32),
        in_specs=[VMEM, VMEM],
        out_specs=VMEM,
        scratch_shapes=[
            pltpu.VMEM((2, ny) + half[1:], f32),
            pltpu.VMEM(half, f32),
            pltpu.VMEM((2, ny) + half[1:], f32),
            dma((2, 4 * (ny - 1))),
        ],
        compiler_params=params(collective_id=1, has_side_effects=True),
        name="column_join",
    )(col_lse, log_b.reshape(col_shape))

    partial, f_out, g_out = pl.pallas_call(
        bary_kernel,
        out_shape=(
            jax.ShapeDtypeStruct((row_tiles + 1, PIECES, width + 8, PIECE), f32),
            jax.ShapeDtypeStruct(row_shape, f32),
            jax.ShapeDtypeStruct(col_shape, f32),
        ),
        in_specs=[ANY, VMEM, VMEM, VMEM, VMEM],
        out_specs=(VMEM, HBM, HBM),
        scratch_shapes=[pltpu.SMEM(rest.shape, i32)]
        + [pltpu.VMEM((TILE, LANES), bf16)] * 3
        + [
            pltpu.VMEM((BARY_GROUP, TILE, TILE), f32),
            pltpu.VMEM((BARY_GROUP, TILE, TILE), bf16),
            dma((3,)),
        ],
        compiler_params=params(),
        name="bary_pass",
    )(rest, points_x, points_y, f_pot, g_pot)

    barycenter = pl.pallas_call(
        functools.partial(bary_join_kernel, gy_size),
        out_shape=jax.ShapeDtypeStruct((rows, width), f32),
        in_specs=[ANY] * 2 + [VMEM] * 5,
        out_specs=VMEM,
        scratch_shapes=[pltpu.SMEM(slots.shape, i32), pltpu.SMEM(slots.shape, f32), dma((2,))]
        + [pltpu.VMEM((TILE, LANES), bf16)] * 3
        + [
            pltpu.VMEM((col_tiles, 1, LANES), f32),
            pltpu.VMEM((2 * SLOTS, TILE, TILE), f32),
            pltpu.VMEM((2 * SLOTS, TILE, TILE), bf16),
            pltpu.VMEM((row_tiles, PIECES, width + 8, PIECE), f32),
            pltpu.VMEM((4, PIECES, width + 8, PIECE), f32),
        ]
        + [pltpu.VMEM((PIECES, width + 8, PIECE), f32)] * 3
        + [dma((2, 4 + 15 * PIECES))],
        compiler_params=params(collective_id=2, has_side_effects=True),
        name="bary_join",
    )(slots, biases, points_x, points_y.reshape(col_tiles, TILE, width), f_pot, g_pot, partial)
    return (f_out.reshape(-1), g_out.reshape(-1), barycenter)


def solution(mesh):
    in_specs = (P("gx", None), P("gy", None), P("gy"), P("gx"), P("gy"), P("gx", None), P("gx"))
    out_specs = (P("gx"), P("gy"), P("gx", None))
    body = functools.partial(local, mesh.shape["gx"], mesh.shape["gy"])
    return jax.shard_map(body, mesh=mesh, in_specs=in_specs, out_specs=out_specs, check_vma=False)
```

```python
import functools

import jax
import jax.numpy as jnp
from jax import lax
from jax.experimental import pallas as pl
from jax.experimental.pallas import tpu as pltpu
from jax.sharding import PartitionSpec as P

TILE = 512
LANES = 128
CHUNKS = TILE // LANES
LSE_GROUP = 2
BARY_GROUP = 2
PIECES = 4
PIECE = TILE // PIECES
PIECE_LANES = [slice(k * PIECE, (k + 1) * PIECE) for k in range(PIECES)]
SLOTS = 2
MESH = pl.DeviceIdType.MESH
NEG_FILL = -1e30
SCALE = 2.8853900817779268
VMEM = pl.BlockSpec(memory_space=pltpu.VMEM)
SMEM = pl.BlockSpec(memory_space=pltpu.SMEM)
HBM = pl.BlockSpec(memory_space=pltpu.HBM)
ANY = pl.BlockSpec(memory_space=pl.ANY)
VMEM_LIMIT = 40 * 1024 * 1024


def params(**kw):
    return pltpu.CompilerParams(vmem_limit_bytes=VMEM_LIMIT, **kw)


def split3(value):
    high = value.astype(jnp.bfloat16).astype(jnp.float32)
    rest = value - high
    middle = rest.astype(jnp.bfloat16).astype(jnp.float32)
    low = (rest - middle).astype(jnp.bfloat16).astype(jnp.float32)
    return [high, middle, low]


def tile_rows(ref, tiles):
    return jnp.concatenate(
        [ref[pl.ds(q, tiles, stride=CHUNKS), :] for q in range(CHUNKS)], axis=1
    )


def as_columns(pieces):
    rows = sum(piece.shape[0] for piece in pieces)
    pieces = pieces + [jnp.zeros((LANES - rows, TILE), jnp.float32)]
    return jnp.concatenate(pieces, axis=0).T.astype(jnp.bfloat16)


def lane_mask(first, period, which):
    lane = lax.broadcasted_iota(jnp.int32, (1, LANES), 1) - first
    hit = (lane == which) | (lane == which + period) | (lane == which + 2 * period)
    return jnp.where(hit, 1.0, 0.0)


def spread(row):
    return jnp.broadcast_to(row, (TILE, LANES)).astype(jnp.bfloat16)


def tile_at(ref, index):
    return ref[pl.ds(pl.multiple_of(index * TILE, TILE), TILE), :]


def product(left, right):
    return lax.dot_general(
        left, right, (((1,), (1,)), ((), ())), preferred_element_type=jnp.float32
    )


def pair_at(list_ref, live, at):
    return list_ref[jnp.minimum(at, live - 1)]


def pipelined(size, live, fill, drain, add=None):
    groups = lax.div(live + (size - 1), size)

    def step(group, carry):
        if add is not None:
            add(group - 1)
        drain(group)
        fill(group + 1)
        return carry

    if add is None:

        @pl.when(groups > 0)
        def _():
            fill(0)
            lax.fori_loop(0, groups - 1, step, 0)
            drain(groups - 1)

        return

    @pl.when(groups > 1)
    def _():
        fill(0)
        drain(0)
        fill(1)
        lax.fori_loop(1, groups - 1, step, 0)
        add(groups - 2)
        drain(groups - 1)
        add(groups - 1)

    @pl.when(groups == 1)
    def _():
        fill(0)
        drain(0)
        add(0)


def fold_rows(value, op):
    rows, lanes = value.shape
    return op(op(value.reshape(4, rows // 32, 8, lanes), axis=1), axis=0)


def lse_pass(
    list_ref, live, pick, outer_ref, inner_ref, pot_tiles, columns, peak, mass, sums, tops
):
    peak[...] = jnp.full_like(peak, NEG_FILL)
    mass[...] = jnp.zeros_like(mass)
    spare = peak.shape[0] - 1

    def fill(group):
        for u in range(LSE_GROUP):
            outer, inner = pick(pair_at(list_ref, live, group * LSE_GROUP + u))
            left = jnp.concatenate([tile_at(outer_ref, outer), columns[...]], axis=1)
            right = jnp.concatenate(
                [tile_at(inner_ref, inner), spread(lane_mask(0, pot_tiles, outer))], axis=1
            )
            value = product(left, right)
            sums[u] = value
            tops[u] = fold_rows(value, jnp.max)

    def drain(group):
        for u in range(LSE_GROUP):
            at = group * LSE_GROUP + u
            inner = jnp.where(at < live, pick(pair_at(list_ref, live, at))[1], spare)
            before = peak[inner]
            top = jnp.maximum(before, tops[u])
            value = sums[u].reshape(TILE // 8, 8, TILE) - top[None]
            terms = fold_rows(jnp.exp2(value * SCALE).reshape(TILE, TILE), jnp.sum)
            mass[inner] = mass[inner] * jnp.exp2((before - top) * SCALE) + terms
            peak[inner] = top

    pipelined(LSE_GROUP, live, fill, drain)


def lse_finish(peak, mass, out_ref):
    for tile in range(peak.shape[0] - 1):
        top = jnp.max(peak[tile], axis=0, keepdims=True)
        total = jnp.sum(mass[tile] * jnp.exp2((peak[tile] - top) * SCALE), axis=0, keepdims=True)
        lse = jnp.where(total > 0.0, 2.0 * top + jnp.log(total), NEG_FILL)
        for q in range(CHUNKS):
            out_ref[pl.ds(tile * CHUNKS + q, 1), :] = lse[:, q * LANES : (q + 1) * LANES]


def row_kernel(
    cols_hbm,
    counts_hbm,
    g_hbm,
    y_hbm,
    x_hbm,
    peak,
    mass,
    list_any,
    rest_any,
    slot_any,
    bias_any,
    x_ref,
    y_ref,
    list_ref,
    rest_ref,
    slot_ref,
    bias_ref,
    cols_ref,
    counts_ref,
    g_ref,
    sems,
    columns,
    *sums,
):
    arrivals = [(cols_hbm, cols_ref), (counts_hbm, counts_ref), (g_hbm, g_ref)]
    arrivals += [(y_hbm, y_ref), (x_hbm, x_ref)]
    copies = [
        pltpu.make_async_copy(src, dst, sems.at[i]) for i, (src, dst) in enumerate(arrivals)
    ]
    for copy in copies:
        copy.start()
    row_tiles, most = cols_ref.shape
    col_tiles = y_ref.shape[0] // TILE
    me = lax.axis_index("gy")
    for copy in copies[:3]:
        copy.wait()
    columns[...] = as_columns(split3(tile_rows(g_ref, col_tiles)))
    live, others = jnp.int32(0), jnp.int32(0)
    for row in range(row_tiles):
        count = counts_ref[row]
        base = (row - me) * col_tiles
        first = live
        for slot in range(most):
            pair = cols_ref[row, slot] + base
            owned = (pair >= row * col_tiles) & (pair < (row + 1) * col_tiles) & (slot < count)
            list_ref[live] = pair
            if slot >= SLOTS:
                rest_ref[others] = pair
                others = others + jnp.where(owned & (live - first >= SLOTS), 1, 0)
            live = live + jnp.where(owned, 1, 0)
        for slot in range(SLOTS):
            here = first + slot < live
            pair = list_ref[first + slot]
            slot_ref[row * SLOTS + slot] = jnp.where(here, pair - row * col_tiles, 0)
            bias_ref[row * SLOTS + slot] = jnp.where(here, 0.0, NEG_FILL)
    list_ref[row_tiles * most + SLOTS] = live
    rest_ref[row_tiles * most] = others
    leaving = [(list_ref, list_any), (rest_ref, rest_any), (slot_ref, slot_any)]
    leaving += [(bias_ref, bias_any)]
    leaving = [
        pltpu.make_async_copy(src, dst, sems.at[5 + i]) for i, (src, dst) in enumerate(leaving)
    ]
    for copy in leaving:
        copy.start()
    copies[3].wait()
    copies[4].wait()
    pick = lambda pair: (lax.rem(pair, col_tiles), lax.div(pair, col_tiles))
    lse_pass(list_ref, live, pick, y_ref, x_ref, col_tiles, columns, peak, mass, *sums)
    for copy in leaving:
        copy.wait()


def column_kernel(
    list_any, x_ref, y_ref, f_ref, peak, mass, list_ref, sem, columns, *sums
):
    fetch = pltpu.make_async_copy(list_any, list_ref, sem)
    fetch.start()
    row_tiles = x_ref.shape[0] // TILE
    col_tiles = y_ref.shape[0] // TILE
    columns[...] = as_columns(split3(tile_rows(f_ref, row_tiles)))
    fetch.wait()
    live = list_ref[list_ref.shape[0] - 1]
    pick = lambda pair: (lax.div(pair, col_tiles), lax.rem(pair, col_tiles))
    lse_pass(list_ref, live, pick, x_ref, y_ref, row_tiles, columns, peak, mass, *sums)


def bary_potentials(f_ref, g_ref, row_tiles, col_tiles, columns, pots_g, pots_f):
    first = 3 * col_tiles
    pots = split3(tile_rows(g_ref, col_tiles)) + split3(tile_rows(f_ref, row_tiles))
    columns[...] = as_columns(pots)
    lane = lax.broadcasted_iota(jnp.int32, (1, LANES), 1)
    pots_g[...] = columns[...] * spread(jnp.where(lane < first, 1.0, 0.0))
    pots_f[...] = columns[...] * spread(jnp.where(lane < first, 0.0, 1.0)) + spread(
        jnp.where(lane == first + 3 * row_tiles, 1.0, 0.0)
    )


def bary_sums(x_tile, y_tile, pots_g, pots_f, row_mask, col_mask):
    left = jnp.concatenate([y_tile, pots_g[...] + spread(row_mask)], axis=1)
    right = jnp.concatenate([x_tile, pots_f[...] + spread(col_mask)], axis=1)
    return product(left, right)


def weighted(points, weights):
    return lax.dot_general(
        points, weights, (((0,), (0,)), ((), ())), preferred_element_type=jnp.float32
    )


def bary_kernel(
    list_any,
    x_ref,
    y_ref,
    f_ref,
    g_ref,
    out_ref,
    f_hbm,
    g_hbm,
    list_ref,
    columns,
    pots_g,
    pots_f,
    sums,
    rounded,
    sems,
):
    fetch = pltpu.make_async_copy(list_any, list_ref, sems.at[2])
    fetch.start()
    results = [
        pltpu.make_async_copy(f_ref, f_hbm, sems.at[0]),
        pltpu.make_async_copy(g_ref, g_hbm, sems.at[1]),
    ]
    for copy in results:
        copy.start()
    row_tiles = x_ref.shape[0] // TILE
    col_tiles = y_ref.shape[0] // TILE
    width = x_ref.shape[1]
    bary_potentials(f_ref, g_ref, row_tiles, col_tiles, columns, pots_g, pots_f)
    out_ref[...] = jnp.zeros_like(out_ref)
    fetch.wait()
    live = list_ref[list_ref.shape[0] - 1]
    spare = out_ref.shape[0] - 1
    pick = lambda pair: (lax.div(pair, col_tiles), lax.rem(pair, col_tiles))

    def fill(group):
        for u in range(BARY_GROUP):
            row, col = pick(pair_at(list_ref, live, group * BARY_GROUP + u))
            row_mask = lane_mask(3 * col_tiles, row_tiles, row)
            col_mask = lane_mask(0, col_tiles, col)
            x_tile, y_tile = tile_at(x_ref, row), tile_at(y_ref, col)
            sums[u] = bary_sums(x_tile, y_tile, pots_g, pots_f, row_mask, col_mask)

    def drain(group):
        for u in range(BARY_GROUP):
            at = group * BARY_GROUP + u
            row = jnp.where(at < live, pick(pair_at(list_ref, live, at))[0], spare)
            weights = jnp.exp2(sums[u] * SCALE)
            mass = fold_rows(weights, jnp.sum)
            for k, lanes in enumerate(PIECE_LANES):
                out_ref[row, k, width:] += mass[:, lanes]
            rounded[u] = weights.astype(jnp.bfloat16)

    def add(group):
        for u in range(BARY_GROUP):
            at = group * BARY_GROUP + u
            row, col = pick(pair_at(list_ref, live, at))
            row = jnp.where(at < live, row, spare)
            total = weighted(tile_at(y_ref, col), rounded[u])
            for k, lanes in enumerate(PIECE_LANES):
                out_ref[row, k, :width] += total[:, lanes]

    pipelined(BARY_GROUP, live, fill, drain, add)
    for copy in results:
        copy.wait()


def meet(peers, work):
    barrier = pltpu.get_barrier_semaphore()
    for peer in peers:
        pl.semaphore_signal(barrier, inc=1, device_id=peer, device_id_type=MESH)
    work()
    pl.semaphore_wait(barrier, len(peers))


def send(src, dst, send_sem, recv_sem, peer):
    copy = pltpu.make_async_remote_copy(
        src_ref=src,
        dst_ref=dst,
        send_sem=send_sem,
        recv_sem=recv_sem,
        device_id=peer,
        device_id_type=MESH,
    )
    copy.start()
    return copy


def join(parts):
    top = parts[0]
    for part in parts[1:]:
        top = jnp.maximum(top, part)
    total = jnp.exp(parts[0] - top)
    for part in parts[1:]:
        total = total + jnp.exp(part - top)
    return top + jnp.log(total)


def row_join_kernel(n, peak, mass, log_a_ref, f_ref, lse_ref, held, send_sem, recv_sem):
    me = lax.axis_index("gy")
    peers = [{"gy": lax.rem(me + d, n)} for d in range(1, n)]
    meet(peers, lambda: lse_finish(peak, mass, lse_ref))
    copies = [
        send(lse_ref, held.at[me], send_sem.at[i], recv_sem.at[i], peer)
        for i, peer in enumerate(peers)
    ]
    held[me] = lse_ref[...]
    for copy in copies:
        copy.wait_recv()
    f_ref[...] = 0.5 * (log_a_ref[...] - join([held[k] for k in range(n)]))
    for copy in copies:
        copy.wait_send()


def col_join_kernel(
    nz, ny, peak, mass, log_b_ref, g_ref, lse_ref, first, part, second, sems
):
    me = lax.axis_index("gx")
    z, y = lax.div(me, ny), lax.rem(me, ny)
    y_peers = [{"gx": z * ny + lax.rem(y + d, ny)} for d in range(1, ny)]
    z_peers = [{"gx": lax.rem(z + d, nz) * ny + y} for d in range(1, nz)]
    meet(y_peers + z_peers, lambda: lse_finish(peak, mass, lse_ref))
    half = lse_ref.shape[0] // 2
    copies = []

    def give(stage, upper):
        held = (first, second)[stage]
        own = lse_ref.at[pl.ds(upper * half, half)] if stage == 0 else part.at[upper]
        at, peers = (y, y_peers) if upper == stage else (z, z_peers)
        given = []
        for peer in peers:
            k = len(copies)
            copy = send(own, held.at[upper, at], sems.at[0, k], sems.at[1, k], peer)
            copies.append(copy)
            given.append(copy)
        held[upper, at] = own[...]
        return given

    def joined(stage, upper, given):
        for copy in given:
            copy.wait_recv()
        return join([(first, second)[stage][upper, k] for k in range(ny)])

    given = [give(0, upper) for upper in range(2)]
    for upper in range(2):
        part[upper] = joined(0, upper, given[upper])
        given[upper] = give(1, upper)
    for upper in range(2):
        rows = slice(upper * half, (upper + 1) * half)
        g_ref[rows] = 0.5 * (log_b_ref[rows] - joined(1, upper, given[upper]))
    for copy in copies:
        copy.wait_send()


def bary_join_kernel(
    n,
    slot_any,
    bias_any,
    x_ref,
    y_ref,
    f_ref,
    g_ref,
    part_ref,
    out_ref,
    slot_ref,
    bias_ref,
    here,
    columns,
    pots_g,
    pots_f,
    masks,
    sums,
    rounded,
    whole,
    near,
    relay,
    left_in,
    right_in,
    sems,
):
    me = lax.axis_index("gy")
    chips = n // 2
    chip, core = lax.div(me, 2), lax.rem(me, 2)
    other = 1 - core
    width = out_ref.shape[1]
    row_tiles, col_tiles = x_ref.shape[0] // TILE, y_ref.shape[0]
    split = width // 2
    low, high = slice(0, split), slice(split, width + 8)
    places = [lax.rem(chip + d, chips) for d in range(chips)]
    sibling = {"gy": chip * 2 + other}
    right, left = {"gy": places[1] * 2 + core}, {"gy": places[3] * 2 + core}
    barrier = pltpu.get_barrier_semaphore()
    for peer in (sibling, right, left):
        pl.semaphore_signal(barrier, inc=1, device_id=peer, device_id_type=MESH)
    fetches = [
        pltpu.make_async_copy(slot_any, slot_ref, here.at[0]),
        pltpu.make_async_copy(bias_any, bias_ref, here.at[1]),
    ]
    for fetch in fetches:
        fetch.start()
    bary_potentials(f_ref, g_ref, row_tiles, col_tiles, columns, pots_g, pots_f)
    lane = lax.broadcasted_iota(jnp.int32, (1, LANES), 1)
    bias_lane = jnp.where(lane == 3 * (col_tiles + row_tiles), 1.0, 0.0)
    for col in range(col_tiles):
        masks[col] = lane_mask(0, col_tiles, col)
    for fetch in fetches:
        fetch.wait()

    def take(rows):
        cols = []
        for i, row in enumerate(rows):
            row_mask = lane_mask(3 * col_tiles, row_tiles, row)
            for k in range(SLOTS):
                col = slot_ref[row * SLOTS + k]
                cols.append(col)
                sums[i * SLOTS + k] = bary_sums(
                    tile_at(x_ref, row),
                    y_ref[col],
                    pots_g,
                    pots_f,
                    row_mask + bias_lane * bias_ref[row * SLOTS + k],
                    masks[col],
                )
        for i, row in enumerate(rows):
            mass = 0.0
            for k in range(i * SLOTS, (i + 1) * SLOTS):
                weights = jnp.exp2(sums[k] * SCALE)
                mass = mass + fold_rows(weights, jnp.sum)
                rounded[k] = weights.astype(jnp.bfloat16)
            for k, lanes in enumerate(PIECE_LANES):
                whole[row, k, width:] = part_ref[row, k, width:] + mass[:, lanes]
        for i, row in enumerate(rows):
            total = 0.0
            for k in range(i * SLOTS, (i + 1) * SLOTS):
                total = total + weighted(y_ref[cols[k]], rounded[k])
            for k, lanes in enumerate(PIECE_LANES):
                whole[row, k, :width] = part_ref[row, k, :width] + total[:, lanes]

    used, copies = [0], []

    def go(src, dst, peer):
        k = used[0]
        used[0] += 1
        copy = send(src, dst, sems.at[0, k], sems.at[1, k], peer)
        copies.append(copy)
        return copy

    def tile(d, kind):
        return places[d] * 2 + kind

    pieces = list(range(PIECES))
    inside, waits = {}, []

    def give_inside(d):
        inside[d] = go(whole.at[tile(d, other)], near.at[d], sibling)

    def add_inside(d):
        inside[d].wait_recv()
        near[d] = near[d] + whole[tile(d, core)]

    take([tile(2, other)])
    pl.semaphore_wait(barrier, 3)
    give_inside(2)
    take([tile(2, core)])
    add_inside(2)
    far = []
    for piece in pieces:
        far.append(
            (
                go(near.at[2, piece, low], relay.at[piece, low], right),
                go(near.at[2, piece, high], relay.at[piece, high], left),
            )
        )
    take([tile(1, other), tile(3, other)])
    give_inside(1)
    give_inside(3)
    take([tile(1, core), tile(3, core)])
    add_inside(1)
    add_inside(3)
    direct, passed = [], []

    def give_direct(piece):
        direct.append(
            (
                go(near.at[1, piece, high], left_in.at[piece, high], right),
                go(near.at[3, piece, low], right_in.at[piece, low], left),
            )
        )

    for piece in pieces[:2]:
        give_direct(piece)
    take([tile(0, other), tile(0, core)])
    give_inside(0)
    for k, piece in enumerate(pieces):
        far[k][0].wait_recv()
        near[1, piece, low] = near[1, piece, low] + relay[piece, low]
        to_right = go(near.at[1, piece, low], left_in.at[piece, low], right)
        far[k][1].wait_recv()
        near[3, piece, high] = near[3, piece, high] + relay[piece, high]
        to_left = go(near.at[3, piece, high], right_in.at[piece, high], left)
        passed.append((to_right, to_left))
        for ahead in pieces[k + 2 : k + 3]:
            give_direct(ahead)
    add_inside(0)

    def rows_of(place, kind, first, count):
        start = (place * 2 + kind) * TILE + first
        return out_ref.at[pl.ds(pl.multiple_of(start, 8), count)]

    size = TILE // PIECES
    own = []
    for k, piece in enumerate(pieces):
        for copy in direct[k] + passed[k]:
            copy.wait_recv()
        total = near[0, k] + left_in[k] + right_in[k]
        ratio = total[:width] / jnp.sum(total[width:], axis=0, keepdims=True)
        mine = rows_of(chip, core, k * size, size)
        mine[...] = ratio.T
        own.append((go(mine, mine, right), go(mine, mine, left)))
        waits.append(go(mine, mine, sibling))
    onward = []
    for k in range(PIECES):
        for side in range(2):
            own[k][side].wait_recv()
            place = places[3] if side == 0 else places[1]
            block = rows_of(place, core, k * size + side * size // 2, size // 2)
            onward.append((k, side, go(block, block, right if side == 0 else left)))
            block = rows_of(place, core, k * size, size)
            waits.append(go(block, block, sibling))
    for k, side, copy in onward:
        copy.wait_recv()
        block = rows_of(places[2], core, k * size + side * size // 2, size // 2)
        waits.append(go(block, block, sibling))
    for copy in waits:
        copy.wait_recv()
    for copy in copies:
        copy.wait_send()


def local(gx_size, gy_size, points_x, points_y, g_init, log_a, log_b, tile_cols, tile_counts):
    row_tiles, most = tile_cols.shape
    rows, width = points_x.shape
    cols = points_y.shape[0]
    col_tiles = cols // TILE
    nz = 1
    while nz * nz < gx_size:
        nz *= 2
    ny = gx_size // nz
    f32, i32, bf16 = jnp.float32, jnp.int32, jnp.bfloat16
    row_shape, col_shape = (rows // LANES, LANES), (cols // LANES, LANES)
    dma = pltpu.SemaphoreType.DMA

    lse_scratch = [
        pltpu.VMEM((TILE, LANES), bf16),
        pltpu.VMEM((LSE_GROUP, TILE, TILE), f32),
        pltpu.VMEM((LSE_GROUP, 8, TILE), f32),
    ]

    sources = (tile_cols, tile_counts, g_init.reshape(col_shape), points_y, points_x)
    lists = (
        ((row_tiles * most + SLOTS + 1,), i32),
        ((row_tiles * most + 1,), i32),
        ((row_tiles * SLOTS,), i32),
        ((row_tiles * SLOTS,), f32),
    )
    row_peak, row_mass, pairs, rest, slots, biases, points_x, points_y = pl.pallas_call(
        row_kernel,
        out_shape=(
            *[pltpu.VMEM((row_tiles + 1, 8, TILE), f32)] * 2,
            *[jax.ShapeDtypeStruct(*a) for a in lists],
            pltpu.VMEM(points_x.shape, bf16),
            pltpu.VMEM(points_y.shape, bf16),
        ),
        in_specs=[HBM] * 5,
        out_specs=(VMEM, VMEM, ANY, ANY, ANY, ANY, VMEM, VMEM),
        scratch_shapes=[pltpu.SMEM(*a) for a in lists]
        + [
            pltpu.SMEM(tile_cols.shape, i32),
            pltpu.SMEM(tile_counts.shape, i32),
            pltpu.VMEM(col_shape, f32),
            dma((9,)),
        ]
        + lse_scratch,
        compiler_params=params(),
        name="row_pass",
    )(*[pltpu.with_memory_space_constraint(source, pltpu.HBM) for source in sources])

    f_pot = pl.pallas_call(
        functools.partial(row_join_kernel, gy_size),
        out_shape=jax.ShapeDtypeStruct(row_shape, f32),
        in_specs=[VMEM] * 3,
        out_specs=VMEM,
        scratch_shapes=[
            pltpu.VMEM(row_shape, f32),
            pltpu.VMEM((gy_size,) + row_shape, f32),
            dma((gy_size - 1,)),
            dma((gy_size - 1,)),
        ],
        compiler_params=params(collective_id=0, has_side_effects=True),
        name="row_join",
    )(row_peak, row_mass, log_a.reshape(row_shape))

    col_peak, col_mass = pl.pallas_call(
        column_kernel,
        out_shape=[pltpu.VMEM((col_tiles + 1, 8, TILE), f32)] * 2,
        in_specs=[ANY, VMEM, VMEM, VMEM],
        out_specs=[VMEM] * 2,
        scratch_shapes=[pltpu.SMEM(pairs.shape, i32), dma] + lse_scratch,
        compiler_params=params(),
        name="column_pass",
    )(pairs, points_x, points_y, f_pot)

    half = (2, col_shape[0] // 2, LANES)
    g_pot = pl.pallas_call(
        functools.partial(col_join_kernel, nz, ny),
        out_shape=jax.ShapeDtypeStruct(col_shape, f32),
        in_specs=[VMEM] * 3,
        out_specs=VMEM,
        scratch_shapes=[
            pltpu.VMEM(col_shape, f32),
            pltpu.VMEM((2, ny) + half[1:], f32),
            pltpu.VMEM(half, f32),
            pltpu.VMEM((2, ny) + half[1:], f32),
            dma((2, 4 * (ny - 1))),
        ],
        compiler_params=params(collective_id=1, has_side_effects=True),
        name="column_join",
    )(col_peak, col_mass, log_b.reshape(col_shape))

    partial, f_out, g_out = pl.pallas_call(
        bary_kernel,
        out_shape=(
            jax.ShapeDtypeStruct((row_tiles + 1, PIECES, width + 8, PIECE), f32),
            jax.ShapeDtypeStruct(row_shape, f32),
            jax.ShapeDtypeStruct(col_shape, f32),
        ),
        in_specs=[ANY, VMEM, VMEM, VMEM, VMEM],
        out_specs=(VMEM, HBM, HBM),
        scratch_shapes=[pltpu.SMEM(rest.shape, i32)]
        + [pltpu.VMEM((TILE, LANES), bf16)] * 3
        + [
            pltpu.VMEM((BARY_GROUP, TILE, TILE), f32),
            pltpu.VMEM((BARY_GROUP, TILE, TILE), bf16),
            dma((3,)),
        ],
        compiler_params=params(),
        name="bary_pass",
    )(rest, points_x, points_y, f_pot, g_pot)

    barycenter = pl.pallas_call(
        functools.partial(bary_join_kernel, gy_size),
        out_shape=jax.ShapeDtypeStruct((rows, width), f32),
        in_specs=[ANY] * 2 + [VMEM] * 5,
        out_specs=VMEM,
        scratch_shapes=[pltpu.SMEM(slots.shape, i32), pltpu.SMEM(slots.shape, f32), dma((2,))]
        + [pltpu.VMEM((TILE, LANES), bf16)] * 3
        + [
            pltpu.VMEM((col_tiles, 1, LANES), f32),
            pltpu.VMEM((2 * SLOTS, TILE, TILE), f32),
            pltpu.VMEM((2 * SLOTS, TILE, TILE), bf16),
            pltpu.VMEM((row_tiles, PIECES, width + 8, PIECE), f32),
            pltpu.VMEM((4, PIECES, width + 8, PIECE), f32),
        ]
        + [pltpu.VMEM((PIECES, width + 8, PIECE), f32)] * 3
        + [dma((2, 4 + 15 * PIECES))],
        compiler_params=params(collective_id=2, has_side_effects=True),
        name="bary_join",
    )(slots, biases, points_x, points_y.reshape(col_tiles, TILE, width), f_pot, g_pot, partial)
    return (f_out.reshape(-1), g_out.reshape(-1), barycenter)


def solution(mesh):
    in_specs = (P("gx", None), P("gy", None), P("gy"), P("gx"), P("gy"), P("gx", None), P("gx"))
    out_specs = (P("gx"), P("gy"), P("gx", None))
    body = functools.partial(local, mesh.shape["gx"], mesh.shape["gy"])
    return jax.shard_map(body, mesh=mesh, in_specs=in_specs, out_specs=out_specs, check_vma=False)
```
